32 devices in a mesh: dp: 8 (over y, x, core), mp: 4 (over z).
Axes of the slice: x: 2, y: 2, z: 4, core: 2. Of those that a mesh axis runs over, the one named last changes fastest.
Arguments:
- tokens: bfloat16 [32768, 768], P(('dp', 'mp')), may hold values from -6 to 6
- segment_ids: int32 [32768], P('dp'), may hold values from 0 to 1, as said below
- row_ends: int32 [128], P('dp'), may hold values from 127 to 255, as said below
- type_rows: bfloat16 [2, 768], replicated, may hold values from -3 to 3
- ln1_gain: float32 [768], replicated, may hold values from 0.1 to 1.9
- attn_qkv: bfloat16 [3, 768, 768], P(None, None, 'mp'), may hold values from -0.21875 to 0.21875
- attn_out: bfloat16 [768, 768], P('mp'), may hold values from -2.5 to 2.5
- ffn_up: bfloat16 [768, 3072], P(None, 'mp'), may hold values from -0.21875 to 0.21875
- ffn_down: bfloat16 [3072, 768], P('mp'), may hold values from -0.109375 to 0.109375
- adapter_down: bfloat16 [16, 768, 48], replicated, may hold values from -0.21875 to 0.21875
- adapter_up: bfloat16 [16, 48, 768], replicated, may hold values from -3 to 3
- ln2_gain: float32 [768], replicated, may hold values from 0.1 to 1.9
- joining_query: bfloat16 [768, 768], P(None, ('dp', 'mp')), may hold values from -0.21875 to 0.21875
- joining_key: bfloat16 [768, 768], P(None, ('dp', 'mp')), may hold values from -0.02734375 to 0.02734375
- joining_value: bfloat16 [768, 768], P(None, ('dp', 'mp')), may hold values from -0.4375 to 0.4375
- query_bias: bfloat16 [768], P(('dp', 'mp')), may hold values from -3 to 3
- cotangent: bfloat16 [32768, 768], P(('dp', 'mp')), may hold values from -6 to 6
Outputs:
- layer_out: float32 [32768, 768], P(('dp', 'mp'))
- grad_input: float32 [32768, 768], P(('dp', 'mp'))
- grad_query: float32 [768, 768], P(None, ('dp', 'mp'))
- grad_key: float32 [768, 768], P(None, ('dp', 'mp'))
- grad_value: float32 [768, 768], P(None, ('dp', 'mp'))
- grad_bias: float32 [768], P(('dp', 'mp'))
The draws below stay inside these ranges and needn't reach their ends.
Inputs may be any that keep to these rules, and one draw needn't show every extreme that they name: A row's tokens after row_ends are padding; segment_ids is 1 from just after a row's first separator (at a position of 1 or more before row_ends) through row_ends and 0 elsewhere; some row ends at 255 and some at 127. `segment_ids`: consistent with row_ends as stated there.
All inputs are finite; a program needn't handle non-finite values.
Results may differ from the reference program's by a relative error of at most 0.034.
Values may be sent and summed in bfloat16 or wider, within the bound.
A program may use at most 256 MiB of HBM per device.

```python
import jax
import jax.numpy as jnp
from jax import lax

D = 768
HEADS = 12
FF = 3072
HEAD = 64
ADAPTERS = 16
BOTTLE = 48
SEQ = 256
SEQ_MB = 4
MICRO = 4
SEQS = 128
TOKENS = 32768


def row_layout(key):
    base = jax.random.fold_in(key, 11)
    first_key, second_key = jax.random.split(base)
    stops = jax.random.randint(first_key, (SEQS,), SEQ // 2 - 1, SEQ)
    stops = stops.at[0].set(SEQ - 1).at[SEQS - 1].set(SEQ // 2 - 1)
    middles = jax.random.randint(second_key, (SEQS,), 1, stops)
    return (stops, middles)


def draw_row_ends(key, part):
    stops, middles = row_layout(key)
    return stops.astype(jnp.int32)


def draw_segment_ids(key, part):
    stops, middles = row_layout(key)
    places = jnp.arange(SEQ, dtype=jnp.int32)[None, :]
    inside = (places > middles[:, None]) & (places <= stops[:, None])
    return inside.astype(jnp.int32).reshape(SEQS * SEQ)


def strengthened(entries, key, source, target, parts, factor):
    owner, partner = [(jnp.arange(entries.shape[axis_at]) // (entries.shape[axis_at] // parts)).reshape([-1 if axis == axis_at else 1 for axis in range(entries.ndim)]) for axis_at in (source, target)]
    chosen = jax.random.permutation(key, parts)[partner]
    strong = (owner == chosen) | (owner == (partner + parts // 2) % parts)
    return jnp.where(strong, factor * entries, entries)


def block_scale(stream_key, extent, pieces, low, largest):
    def one(dim, parts):
        steps = jax.random.uniform(jax.random.fold_in(jax.random.fold_in(stream_key, 6), dim), (parts,), jnp.float32, low / len(pieces), largest / len(pieces))
        return jnp.repeat(jnp.exp(steps), extent[dim] // parts).reshape((-1,) + (1,) * (len(extent) - dim - 1))

    level = one(*pieces[0])
    for cut in pieces[1:]:
        level = level * one(*cut)
    return level


def scatter_about(key, dims, width, bound, cuts=(), held_as=jnp.bfloat16):
    entries = width * jax.random.normal(key, dims, jnp.float32)
    if cuts:
        entries = entries * block_scale(key, dims, cuts, -0.22, 0.18)
    return jnp.clip(entries, -bound, bound).astype(held_as)


def heavy_noise(rng, extent, scale, reach, cuts, heavy, held_as=jnp.bfloat16):
    values = scale * jax.random.normal(rng, extent, jnp.float32)
    if cuts:
        values = values * block_scale(rng, extent, cuts, -0.22, 0.18)
    return jnp.clip(strengthened(values, jax.random.fold_in(rng, 3), *heavy), -reach, reach).astype(held_as)


def setup_inputs(seed: int = 0) -> dict:
    key_of = jax.random.split(jax.random.key(seed), 18)
    tokens = scatter_about(key_of[0], (TOKENS, D), 1.0, 6.0, ((0, 32),))
    segment_ids = draw_segment_ids(jax.random.fold_in(key_of[17], 71), 0)
    row_ends = draw_row_ends(jax.random.fold_in(key_of[17], 71), 0)
    type_rows = scatter_about(key_of[3], (2, D), 0.5, 3.0)
    ln1_gain = jnp.clip(1.0 + 0.18 * jax.random.normal(key_of[4], (D,), jnp.float32), 0.1, 1.9)
    attn_qkv = scatter_about(key_of[5], (3, D, D), D ** -0.5, 0.21875, ((2, 4),))
    attn_out = scatter_about(key_of[6], (D, D), (D // 128) ** -0.5, 2.5, ((0, 4),))
    ffn_up = scatter_about(key_of[7], (D, FF), D ** -0.5, 0.21875, ((1, 4),))
    ffn_down = scatter_about(key_of[8], (FF, D), FF ** -0.5, 0.109375, ((0, 4),))
    adapter_down = scatter_about(key_of[9], (ADAPTERS, D, BOTTLE), D ** -0.5, 0.21875)
    adapter_up = scatter_about(key_of[10], (ADAPTERS, BOTTLE, D), (max(BOTTLE // 12, 1)) ** -0.5, 3.0)
    ln2_gain = jnp.clip(1.0 + 0.18 * jax.random.normal(key_of[11], (D,), jnp.float32), 0.1, 1.9)
    joining_query = scatter_about(key_of[12], (D, D), D ** -0.5, 0.21875, ((1, 32),))
    joining_key = scatter_about(key_of[13], (D, D), (64 * D) ** -0.5, 0.02734375, ((1, 32),))
    joining_value = scatter_about(key_of[14], (D, D), (D // 4) ** -0.5, 0.4375, ((1, 32),))
    query_bias = scatter_about(key_of[15], (D,), 0.5, 3.0, ((0, 32),))
    cotangent = heavy_noise(key_of[16], (TOKENS, D), 1.0, 6.0, ((0, 32),), (0, 1, 32, 2.75))
    return {"tokens": tokens, "segment_ids": segment_ids, "row_ends": row_ends, "type_rows": type_rows, "ln1_gain": ln1_gain, "attn_qkv": attn_qkv, "attn_out": attn_out, "ffn_up": ffn_up, "ffn_down": ffn_down, "adapter_down": adapter_down, "adapter_up": adapter_up, "ln2_gain": ln2_gain, "joining_query": joining_query, "joining_key": joining_key, "joining_value": joining_value, "query_bias": query_bias, "cotangent": cotangent}


@jax.custom_vjp
def low(v):
    return lax.optimization_barrier(v.astype(jnp.bfloat16)).astype(jnp.float32)

@jax.custom_vjp
def low_back(v):
    return v

def low_keep(v):
    return (low(v), None)

def low_pass(kept, grad):
    return (grad,)

def back_keep(v):
    return (v, None)

def back_low(kept, grad):
    return (low(grad),)
low.defvjp(low_keep, low_pass)
low_back.defvjp(back_keep, back_low)
eps = 1e-06
highest = lax.Precision.HIGHEST

def exact_gelu(values):
    return jax.nn.gelu(values, approximate=False)

def layer_norm(values, gain):
    center = values - lax.optimization_barrier(jnp.mean(values, axis=-1, keepdims=True))
    spread = lax.optimization_barrier(jnp.mean(center * center, axis=-1, keepdims=True))
    return gain * (center * lax.rsqrt(spread + eps))

def matmul(left, right):
    return jnp.dot(left, right, precision=highest, preferred_element_type=jnp.float32)

def block_forward(frozen, trained, inputs, segments, seq_ends):
    type_rows, ln1_gain, attn_qkv, attn_out, ffn_up, ffn_down, adapter_down, adapter_up, ln2_gain = frozen
    joining_query, joining_key, joining_value, query_bias = trained
    seq_count = seq_ends.shape[0]
    summed = inputs + jnp.where(segments[:, None] == 1, type_rows[1][None, :], type_rows[0][None, :])
    rounded = low(summed)
    triple = [low(low_back(matmul(rounded, attn_qkv[member]))).reshape(seq_count, SEQ, HEADS, HEAD) for member in range(3)]
    queries, key_rows, val_rows = triple
    scores = low_back(jnp.einsum('sqhd,skhd->shqk', queries, key_rows, precision=highest) * HEAD ** (-0.5))
    places = jnp.arange(SEQ, dtype=jnp.int32)
    valid = places[None, None, None, :] <= seq_ends[:, None, None, None]
    scores = jnp.where(valid, scores, -1e+30)
    probs = low(jax.nn.softmax(scores, axis=-1))
    context = low(low_back(jnp.einsum('shqk,skhd->sqhd', probs, val_rows, precision=highest))).reshape(seq_count * SEQ, D)
    attended = low_back(matmul(context, attn_out))
    hidden_one = layer_norm(summed + attended, ln1_gain)
    widened = low_back(matmul(low(hidden_one), ffn_up))
    activated = low(exact_gelu(widened))
    branch = low_back(matmul(activated, ffn_down))
    merged = hidden_one + branch
    merged_low = low(merged)
    adapt_pre = low_back(jnp.einsum('rd,adb->rab', merged_low, adapter_down, precision=highest))
    adapt_mid = low(exact_gelu(adapt_pre))
    adapted = low(low_back(merged[:, None, :] + jnp.einsum('rab,abd->rad', adapt_mid, adapter_up, precision=highest)))
    query_rows = low(low_back(matmul(merged_low, joining_query) + query_bias[None, :]))
    keyed = low(low_back(jnp.einsum('rd,ed->re', query_rows, joining_key, precision=highest)))
    joining_scores = jnp.einsum('re,rae->ra', keyed, adapted, precision=highest) * D ** (-0.5)
    joining_probs = low(jax.nn.softmax(joining_scores, axis=-1))
    mixed = low(jnp.einsum('ra,rad->rd', joining_probs, adapted, precision=highest))
    joined = low_back(matmul(mixed, joining_value))
    return layer_norm(merged + joined, ln2_gain)

def reference(tokens, segment_ids, row_ends, type_rows, ln1_gain, attn_qkv, attn_out, ffn_up, ffn_down, adapter_down, adapter_up, ln2_gain, joining_query, joining_key, joining_value, query_bias, cotangent):
    frozen = tuple((member.astype(jnp.float32) for member in (type_rows, ln1_gain, attn_qkv, attn_out, ffn_up, ffn_down, adapter_down, adapter_up, ln2_gain)))
    trained = tuple((member.astype(jnp.float32) for member in (joining_query, joining_key, joining_value, query_bias)))
    block_seqs = SEQ_MB * MICRO
    blocks = SEQS // block_seqs
    block_rows = block_seqs * SEQ
    inputs = tokens.astype(jnp.float32).reshape(blocks, block_rows, D)
    segments = segment_ids.reshape(blocks, block_rows)
    stops = row_ends.reshape(blocks, block_seqs)
    checked = jax.checkpoint(block_forward)

    def whole(inputs_all, trained_all):

        def visit_block(carry, slices):
            return (carry, checked(frozen, trained_all, slices[0], slices[1], slices[2]))
        _, results = lax.scan(visit_block, jnp.zeros((), jnp.float32), (inputs_all, segments, stops))
        return results
    results, pullback = jax.vjp(whole, inputs, trained)
    grad_inputs, grad_trained = pullback(cotangent.astype(jnp.float32).reshape(blocks, block_rows, D))
    layer_out = results.reshape(TOKENS, D).astype(jnp.float32)
    grad_input = grad_inputs.reshape(TOKENS, D).astype(jnp.float32)
    return (layer_out, grad_input, grad_trained[0], grad_trained[1], grad_trained[2], grad_trained[3])
```

```python
import jax
import jax.numpy as jnp
from jax import lax
from jax.sharding import PartitionSpec as P

HEAD = 64
EPS = 1e-06
ROOT_HALF = 0.7071067811865476
INV_ROOT_2PI = 0.3989422804014327


def mm(a, b):
    return jnp.dot(a, b, preferred_element_type=jnp.float32)


def mm_nt(a, b):
    return lax.dot_general(a, b, (((1,), (1,)), ((), ())), preferred_element_type=jnp.float32)


def mm_tn(a, b):
    return lax.dot_general(a, b, (((0,), (0,)), ((), ())), preferred_element_type=jnp.float32)


def low(v):
    return v.astype(jnp.bfloat16)


def gelu_pair(x):
    cdf = 0.5 * (1.0 + lax.erf(x * ROOT_HALF))
    return x * cdf, cdf + x * (INV_ROOT_2PI * jnp.exp(-0.5 * x * x))


def normalize(v):
    center = v - jnp.mean(v, axis=-1, keepdims=True)
    r = lax.rsqrt(jnp.mean(center * center, axis=-1, keepdims=True) + EPS)
    return center * r, r


def norm_back(n, r, t):
    return r * (t - jnp.mean(t, axis=-1, keepdims=True) - n * jnp.mean(t * n, axis=-1, keepdims=True))


def local(
    tokens,
    segment_ids,
    row_ends,
    type_rows,
    ln1_gain,
    attn_qkv,
    attn_out,
    ffn_up,
    ffn_down,
    adapter_down,
    adapter_up,
    ln2_gain,
    joining_query,
    joining_key,
    joining_value,
    query_bias,
    cotangent,
):
    dp, mp = lax.axis_size("dp"), lax.axis_size("mp")
    dpi, mpi = lax.axis_index("dp"), lax.axis_index("mp")
    rows, width = tokens.shape
    seqs = row_ends.shape[0] // mp
    seq_len = rows // seqs
    adapters, _, bottle = adapter_down.shape
    factor = width ** (-0.5)
    scale = HEAD ** (-0.5)

    def share(mat):
        piece = mat.shape[0] // dp
        mine = lax.dynamic_slice_in_dim(mat, dpi * piece, piece, 0)
        return lax.all_gather(mine, ("mp", "dp"), axis=0, tiled=True)

    cols = attn_qkv.shape[2]
    qkv_all = share(jnp.transpose(attn_qkv, (1, 0, 2)).reshape(width, 3 * cols))
    qkv_all = qkv_all.reshape(mp, width, 3 * cols)
    out_all = share(attn_out)
    up_all = share(ffn_up).reshape(mp, width, ffn_up.shape[1])
    down_all = share(ffn_down).reshape(mp, ffn_down.shape[0], width)
    up_mat = adapter_up.reshape(adapters * bottle, width)
    dn_mat = jnp.transpose(adapter_down, (1, 0, 2)).reshape(width, adapters * bottle)

    own_q = jnp.transpose(joining_query)
    own_m = low(mm_nt(jnp.transpose(joining_key), up_mat))
    own_v = jnp.transpose(joining_value)
    q_t = lax.all_gather(own_q, ("dp", "mp"), axis=0, tiled=True)
    m_all = lax.all_gather(own_m, ("dp", "mp"), axis=0, tiled=True)
    v_t = lax.all_gather(own_v, ("dp", "mp"), axis=0, tiled=True)
    bias = lax.all_gather(query_bias, ("dp", "mp"), axis=0, tiled=True)
    w_mat = low(mm_tn(q_t, m_all))
    shift = mm(bias[None, :], m_all)

    own_types = lax.dynamic_slice_in_dim(segment_ids, mpi * rows, rows)
    ends = lax.dynamic_slice_in_dim(row_ends, mpi * seqs, seqs)
    type_f = type_rows.astype(jnp.float32)
    x = tokens.astype(jnp.float32) + jnp.where(
        own_types[:, None] == 1, type_f[1][None, :], type_f[0][None, :]
    )
    xb = low(x)
    heads = cols // HEAD
    proj = low(jnp.einsum("rd,zdc->zrc", xb, qkv_all, preferred_element_type=jnp.float32))
    pieces = proj.reshape(mp, seqs, seq_len, 3, heads, HEAD)
    q, k, v = pieces[:, :, :, 0], pieces[:, :, :, 1], pieces[:, :, :, 2]
    sc = jnp.einsum("zsqhd,zskhd->zshqk", q, k, preferred_element_type=jnp.float32) * scale
    places = lax.broadcasted_iota(jnp.int32, (1, 1, 1, 1, seq_len), 4)
    sc = jnp.where(places <= ends[None, :, None, None, None], sc, -1e30)
    e = jnp.exp(sc - jnp.max(sc, axis=-1, keepdims=True))
    probs = e / jnp.sum(e, axis=-1, keepdims=True)
    pb = low(probs)
    ctx = low(jnp.einsum("zshqk,zskhd->sqzhd", pb, v, preferred_element_type=jnp.float32))
    ctx2 = ctx.reshape(rows, width)
    n1, r1 = normalize(x + mm(ctx2, out_all))
    h1 = n1 * ln1_gain[None, :]
    h1b = low(h1)
    wide = jnp.einsum("rd,zdf->zrf", h1b, up_all, preferred_element_type=jnp.float32)
    act, act_back = gelu_pair(wide)
    act, act_back = low(act), low(act_back)
    merged = h1 + jnp.einsum("zrf,zfd->rd", act, down_all, preferred_element_type=jnp.float32)
    mb = low(merged)

    mid, mid_back = gelu_pair(mm(mb, dn_mat))
    ku = mm(mb, w_mat) + shift

    def group_sum(t):
        return jnp.sum(t.reshape(rows, adapters, bottle), axis=-1)

    def spread(t):
        return jnp.broadcast_to(t[:, :, None], (rows, adapters, bottle)).reshape(rows, adapters * bottle)

    jp = jax.nn.softmax(group_sum(mid * ku) * factor, axis=-1)
    mixed = low(merged + mm(low(spread(jp) * mid), up_mat))
    n2, r2 = normalize(merged + mm_nt(mixed, v_t))
    layer_out = n2 * ln2_gain[None, :]
    gc = norm_back(n2, r2, cotangent.astype(jnp.float32) * ln2_gain[None, :])
    gcb = low(gc)
    grad_value = mm_tn(mixed, gcb)
    gm = mm(gcb, v_t)
    gu = mm_nt(low(gm), up_mat)
    gp = group_sum(mid * gu)
    gs = jp * (gp - jnp.sum(jp * gp, axis=-1, keepdims=True)) * factor
    zb = low(spread(gs) * mid)
    big_r = mm_tn(zb, mb)
    small_s = jnp.sum(zb.astype(jnp.float32), axis=0)
    g_pre = low(mid_back * (spread(jp) * gu + spread(gs) * ku))
    g_merged = gc + gm + mm_nt(zb, w_mat) + mm_nt(g_pre, dn_mat)
    gmb = low(g_merged)
    g_act = jnp.einsum("rd,zfd->zrf", gmb, down_all, preferred_element_type=jnp.float32)
    g_wide = low(g_act * act_back)
    g_hid = g_merged + jnp.einsum("zrf,zdf->rd", g_wide, up_all, preferred_element_type=jnp.float32)
    g_sum = norm_back(n1, r1, g_hid * ln1_gain[None, :])
    g_ctx = low(mm_nt(low(g_sum), out_all)).reshape(seqs, seq_len, mp, heads, HEAD)
    delta = jnp.sum(
        g_ctx.astype(jnp.float32) * ctx.astype(jnp.float32), axis=-1
    )
    gpr = jnp.einsum("sqzhd,zskhd->zshqk", g_ctx, v, preferred_element_type=jnp.float32)
    ds = low(pb.astype(jnp.float32) * (gpr - jnp.transpose(delta, (2, 0, 3, 1))[..., None]))
    gv = low(jnp.einsum("zshqk,sqzhd->zskhd", pb, g_ctx, preferred_element_type=jnp.float32))
    gq = low(jnp.einsum("zshqk,zskhd->zsqhd", ds, k, preferred_element_type=jnp.float32) * scale)
    gk = low(jnp.einsum("zshqk,zsqhd->zskhd", ds, q, preferred_element_type=jnp.float32) * scale)
    g_proj = jnp.stack((gq, gk, gv), axis=3).reshape(mp, rows, 3 * cols)
    g_in = g_sum + jnp.einsum("zrc,zdc->rd", g_proj, qkv_all, preferred_element_type=jnp.float32)

    g_value = lax.psum_scatter(jnp.transpose(low(grad_value)), ("dp", "mp"), scatter_dimension=0, tiled=True)
    packed = jnp.concatenate((low(big_r), low(small_s)[None, :], jnp.zeros((15, width), jnp.bfloat16)))
    total = lax.psum(packed, ("dp", "mp"))
    big_r, small_s = total[:width], total[width]
    g_query = mm_tn(big_r, jnp.transpose(own_m))
    inner = mm(big_r, joining_query) + small_s.astype(jnp.float32)[:, None] * query_bias.astype(jnp.float32)[None, :]
    g_key = mm_tn(up_mat, low(inner))
    g_bias = mm(own_m, small_s[:, None])[:, 0]
    return (layer_out, g_in, g_query, g_key, jnp.transpose(g_value).astype(jnp.float32), g_bias)


def solution(mesh):
    in_specs = (
        P(("dp", "mp"), None),
        P("dp"),
        P("dp"),
        P(),
        P(),
        P(None, None, "mp"),
        P("mp", None),
        P(None, "mp"),
        P("mp", None),
        P(),
        P(),
        P(),
        P(None, ("dp", "mp")),
        P(None, ("dp", "mp")),
        P(None, ("dp", "mp")),
        P(("dp", "mp")),
        P(("dp", "mp"), None),
    )
    out_specs = (
        P(("dp", "mp"), None),
        P(("dp", "mp"), None),
        P(None, ("dp", "mp")),
        P(None, ("dp", "mp")),
        P(None, ("dp", "mp")),
        P(("dp", "mp")),
    )
    return jax.shard_map(local, mesh=mesh, in_specs=in_specs, out_specs=out_specs, check_vma=False)
```

```python
import functools

import jax
import jax.numpy as jnp
from jax import lax
from jax.experimental import pallas as pl
from jax.experimental.pallas import tpu as pltpu
from jax.sharding import PartitionSpec as P

HEAD = 64
EPS = 1e-06
ROOT_HALF = 0.7071067811865476
INV_ROOT_2PI = 0.3989422804014327
NEG = -1e30
MESH = pl.DeviceIdType.MESH
PLANE = 80
BF = jnp.bfloat16
F32 = jnp.float32


def nn(a, b):
    return jnp.dot(a, b, preferred_element_type=F32)


def nt(a, b):
    return lax.dot_general(a, b, (((1,), (1,)), ((), ())), preferred_element_type=F32)


def tn(a, b):
    return lax.dot_general(a, b, (((0,), (0,)), ((), ())), preferred_element_type=F32)


def low(v):
    return v.astype(BF)


def gelu_pair(v):
    cdf = 0.5 + 0.5 * lax.erf(v * ROOT_HALF)
    return v * cdf, cdf + v * (INV_ROOT_2PI * jnp.exp(-0.5 * (v * v)))


def mean(v):
    return jnp.sum(v, axis=-1, keepdims=True) * (1.0 / v.shape[-1])


def normalize(v):
    center = v - mean(v)
    r = lax.rsqrt(mean(center * center) + EPS)
    return center * r, r


def norm_back(n, r, t):
    return r * (t - mean(t) - n * mean(t * n))


def half_mask(h, value):
    lane = lax.broadcasted_iota(jnp.int32, (1, 2 * HEAD), 1)
    inside = (lane >= h * HEAD) & (lane < (h + 1) * HEAD)
    return jnp.where(inside, jnp.asarray(value, F32), jnp.asarray(0.0, F32)).astype(BF)


def flat_row(ref):
    return jnp.concatenate([ref[i : i + 1, :] for i in range(ref.shape[0])], axis=1)


class Mover:
    def __init__(self, send, recv):
        self.send, self.recv, self.count, self.open = send, recv, 0, []

    def slot(self):
        self.count += 1
        return self.count - 1

    def remote(self, src, dst, peer, start=True):
        i = self.slot()
        copy = pltpu.make_async_remote_copy(
            src_ref=src, dst_ref=dst, send_sem=self.send.at[i], recv_sem=self.recv.at[i],
            device_id=peer, device_id_type=MESH,
        )
        copy.start()
        self.open.append(copy)
        return copy

    def local(self, src, dst):
        copy = pltpu.make_async_copy(src, dst, self.send.at[self.slot()])
        copy.start()
        return copy

    def drain(self):
        for copy in self.open:
            copy.wait_send()
        self.open = []


def kernel(
    dims,
    tok_in, cot_in, seg_in, ends_in, type_in, gain1_in, gain2_in, bias_in, qkv_in, out_in, up_in, down_in, adn_in, aup_in, jq_in, jk_in, jv_in,
    layer_out, grad_out, join_out, probs_out, proj_out,
    wq, wo, wu, wd, aup, adn, wmat, mmat, qmat, vmat, shift, jbuf,
    rc, rxa, ryb, rya, rxb, rz,
    ct, proj, big, back, ctx, n1, r1, merged, stage, jprob, own_m,
    send, recv,
):
    rows, width, seqs, seq_len, parts, adapters, bottle, share = dims
    d, z = lax.axis_index("dp"), lax.axis_index("mp")
    p = lax.rem(d, 8)
    c, x, y = lax.rem(p, 2), lax.rem(p // 2, 2), p // 4
    xn = (d + 2 - 4 * x, z)
    yn = (d + 4 - 8 * y, z)
    cn = (d + 1 - 2 * c, z)
    zn = [None] + [(d, lax.rem(z + k, parts)) for k in range(1, parts)]
    q = p // 2
    qx, qy = q + 1 - 2 * x, q + 2 - 4 * y
    qd = qx + 2 - 4 * y
    factor = width ** (-0.5)
    half = width // 2

    barrier = pltpu.get_barrier_semaphore()
    for peer in [xn, yn, cn] + zn[1:]:
        pl.semaphore_signal(barrier, inc=1, device_id=peer, device_id_type=MESH)
    pl.semaphore_wait(barrier, 2 + parts)

    mv = Mover(send, recv)

    class Unit:
        def __init__(self, src, dst, piece, split, needs):
            self.src, self.dst, self.piece, self.split, self.needs = src, dst, piece, split, needs
            self.z, self.x, self.y, self.dx, self.dy, self.cc = {}, {}, {}, {}, {}, {}

        def start(self):
            for k in range(1, parts):
                self.z[parts - k] = mv.remote(self.src, self.dst(k), zn[k])

        def first(self, g):
            for k in self.needs[g]:
                self.z[k].wait_recv()
            ref = self.piece(g, q, c, 0, None)
            self.x[g] = mv.remote(ref, ref, xn)
            self.y[g] = mv.remote(ref, ref, yn)
            self.cc[g, 0] = mv.remote(ref, ref, cn)

        def second(self, g):
            self.x[g].wait_recv()
            part = self.split(0, g)
            if part is not None:
                ref = self.piece(g, qx, c, *part)
                self.dy[g] = mv.remote(ref, ref, yn)
            ref = self.piece(g, qx, c, 0, None)
            self.cc[g, 1] = mv.remote(ref, ref, cn)
            self.y[g].wait_recv()
            part = self.split(1, g)
            if part is not None:
                ref = self.piece(g, qy, c, *part)
                self.dx[g] = mv.remote(ref, ref, xn)
            ref = self.piece(g, qy, c, 0, None)
            self.cc[g, 2] = mv.remote(ref, ref, cn)

        def third(self, g):
            for got in (self.dx, self.dy):
                if g in got:
                    got[g].wait_recv()
            ref = self.piece(g, qd, c, 0, None)
            self.cc[g, 3] = mv.remote(ref, ref, cn)

        def last(self):
            for copy in self.cc.values():
                copy.wait_recv()

    def frozen(src, buf, piece_rows, cut, groups, lead):
        def window(ref, zs, chip, core, off, count):
            count = piece_rows if count is None else count
            at = (zs, pl.ds(chip * piece_rows + off, count), pl.ds(pl.multiple_of(core * half, half), half))
            return ref.at[(slice(None),) * lead + at]

        def own():
            at = (pl.ds(q * piece_rows, piece_rows), pl.ds(pl.multiple_of(c * half, half), half))
            return src.at[(slice(None),) * lead + at]

        return Unit(
            own(),
            lambda k: window(buf, parts - k, q, c, 0, None),
            lambda g, chip, core, off, count: window(buf, pl.ds(*groups[g]), chip, core, off, count),
            lambda which, g: ((0, cut), (cut, piece_rows - cut))[which],
            [range(at, at + count) for at, count in groups],
        )

    heads_rows = wo.shape[1]
    each = [(k, 1) for k in range(1, parts)]
    whole = [(1, parts - 1)]
    u_qkv = frozen(qkv_in, wq, heads_rows // 4, 32, each, 1)
    u_out = frozen(out_in, wo, heads_rows // 4, 16, whole, 0)
    u_up = frozen(up_in, wu, wu.shape[1] // 4, wu.shape[1] // 8, whole, 0)
    u_down = frozen(down_in, wd, wd.shape[1] // 4, wd.shape[1] // 8, whole, 0)
    jg = [(0, parts // 2), (parts // 2, parts // 2)]

    def jpiece(g, chip, core, off, count):
        return jbuf.at[chip // 2, lax.rem(chip, 2), core, pl.ds(*jg[g])]

    u_join = Unit(
        jbuf.at[y, x, c, z],
        lambda k: jbuf.at[y, x, c, z],
        jpiece,
        lambda which, g: (0, None) if which == g else None,
        [range(1, parts), ()],
    )

    u_qkv.start()
    l_up = mv.local(aup_in, aup)
    l_dn = mv.local(adn_in, adn)
    l_qkv = mv.local(qkv_in, wq.at[:, 0])
    l_tok = mv.local(tok_in, ct)
    l_out = mv.local(out_in, wo.at[0])
    l_wu = mv.local(up_in, wu.at[0])
    l_wd = mv.local(down_in, wd.at[0])
    u_out.start()

    gain1, gain2 = flat_row(gain1_in), flat_row(gain2_in)
    spot = lax.broadcasted_iota(jnp.int32, (share, share), 0) == lax.broadcasted_iota(
        jnp.int32, (share, share), 1
    )
    bias_col = jnp.sum(jnp.where(spot, bias_in[...].astype(F32), 0.0), axis=1, keepdims=True)
    l_up.wait()
    m_low = low(nt(jk_in[...], aup[...])).astype(F32)
    own_m[...] = m_low
    part_shift = jnp.sum(bias_col * m_low, axis=0, keepdims=True)
    high = low(part_shift).astype(F32)
    blank = jnp.zeros((PLANE - 3 * share - 2, width), F32)
    tail = jnp.concatenate((high, part_shift - high, blank), axis=0)
    jbuf[y, x, c, z] = low(
        jnp.concatenate((jq_in[...].astype(F32), m_low, jv_in[...].astype(F32), tail), axis=0)
    )
    u_qkv.first(0)
    for g in range(1, parts - 1):
        u_qkv.first(g)
    u_up.start()
    u_out.first(0)
    for g in range(parts - 1):
        u_qkv.second(g)
    for g in range(parts - 1):
        u_qkv.third(g)
    u_out.second(0)
    u_qkv.last()
    u_out.third(0)

    l_tok.wait()
    l_qkv.wait()
    chunks = rows // 128
    seg = seg_in[pl.ds(pl.multiple_of(z * chunks, chunks), chunks), :].astype(F32)
    column = jnp.transpose(seg)
    per_seq = seq_len // 128
    type_f = type_in[...].astype(F32)

    def summed(s):
        rs = pl.ds(s * seq_len, seq_len)
        picks = [column[:, k : k + 1] for k in range(s * per_seq, (s + 1) * per_seq)]
        pick = jnp.concatenate(picks, axis=0) > 0.5
        return ct[rs, :].astype(F32) + jnp.where(pick, type_f[1:2], type_f[0:1])

    xb = jnp.concatenate([low(summed(s)) for s in range(seqs)], axis=0)
    for t in range(3):
        proj[:, t * width : (t + 1) * width] = low(nt(xb, wq[t].reshape(width, width)))
    u_up.first(0)
    u_down.start()

    pairs = width // (2 * HEAD)
    scale = HEAD ** (-0.5)
    probs_copies = []

    def at_pair(hp, t):
        return pl.ds(pl.multiple_of(t * width + hp * 2 * HEAD, 2 * HEAD), 2 * HEAD)

    def prob_ref(s, hp, h):
        head = hp * 2 + h
        per = width // seq_len
        return (
            head // per,
            pl.ds(s * seq_len, seq_len),
            pl.ds(pl.multiple_of(lax.rem(head, per) * seq_len, seq_len), seq_len),
        )

    places = lax.broadcasted_iota(jnp.int32, (1, seq_len), 1)
    for s in range(seqs):
        rs = pl.ds(s * seq_len, seq_len)
        hidden = jnp.where(places <= ends_in[z * seqs + s], 0.0, NEG)

        def one(hp, carry, s=s, rs=rs, hidden=hidden):
            qp, kp, vp = (proj[rs, at_pair(hp, t)] for t in range(3))
            total = None
            for h in range(2):
                sc = nt(qp, kp * half_mask(h, scale)) + hidden
                e = jnp.exp(sc - jnp.max(sc, axis=1, keepdims=True))
                pb = low(e * (1.0 / jnp.sum(e, axis=1, keepdims=True)))
                big[prob_ref(s, hp, h)] = pb
                term = nn(pb, vp * half_mask(h, 1.0))
                total = term if total is None else total + term
            ctx[rs, at_pair(hp, 0)] = low(total)
            return carry

        lax.fori_loop(0, pairs, one, 0, unroll=3)
        probs_copies.append(mv.local(big.at[:, rs], probs_out.at[:, rs]))
        if s == 1:
            u_out.last()
        if s == 2:
            u_up.second(0)

    proj_copy = mv.local(proj, proj_out)

    l_out.wait()
    block = 2 * seq_len
    w_out = wo[...].reshape(width, width)
    for b in range(rows // block):
        rs = pl.ds(b * block, block)
        xs = jnp.concatenate((summed(2 * b), summed(2 * b + 1)), axis=0)
        n, r = normalize(xs + nn(ctx[rs, :], w_out))
        n1[rs, :] = low(n)
        r1[rs, :] = r
        h = n * gain1
        merged[rs, :] = h
        ct[rs, :] = low(h)
    u_up.third(0)
    u_down.first(0)
    u_join.start()
    u_up.last()
    for copy in probs_copies:
        copy.wait()

    l_wu.wait()
    for j in range(parts):
        act, slope = gelu_pair(nn(ct[...], wu[j]))
        big[j] = low(act)
        back[j] = low(slope)
        if j == 1:
            u_down.second(0)
    l_cot = mv.local(cot_in, ct)
    u_join.first(0)
    u_join.first(1)
    u_down.third(0)
    l_wd.wait()
    u_down.last()
    for b in range(rows // block):
        rs = pl.ds(b * block, block)
        total = merged[rs, :]
        for j in range(parts):
            total += nn(big[j, rs, :], wd[j])
        merged[rs, :] = total
        if b == 0:
            u_join.second(0)
            u_join.second(1)
    u_join.third(0)
    u_join.third(1)
    u_join.last()

    piece = parts * share

    def pack(i, total):
        planes = [jbuf[i // 4, lax.rem(i // 2, 2), lax.rem(i, 2), k].astype(F32) for k in range(parts)]
        at = pl.ds(pl.multiple_of(i * piece, piece), piece)
        for n, mat in enumerate((qmat, mmat, vmat)):
            mat[at, :] = low(
                jnp.concatenate([pl_[n * share : (n + 1) * share] for pl_ in planes], axis=0)
            )
        for pl_ in planes:
            total += pl_[3 * share : 3 * share + 1] + pl_[3 * share + 1 : 3 * share + 2]
        return total

    shift[...] = lax.fori_loop(0, 8, pack, jnp.zeros((1, width), F32))
    wmat[...] = low(tn(qmat[...], mmat[...]))
    mv.drain()

    units = adapters * bottle
    row_i = lax.broadcasted_iota(jnp.int32, (units, 128), 0)
    lane_i = lax.broadcasted_iota(jnp.int32, (units, 128), 1)
    gather_mat = low(
        jnp.where((row_i >= lane_i * bottle) & (row_i < (lane_i + 1) * bottle), 1.0, 0.0)
    )
    live = lax.broadcasted_iota(jnp.int32, (1, 128), 1) < adapters
    l_cot.wait()
    l_dn.wait()
    proj_copy.wait()
    mid_at, slope_at, ku_at = (slice(t * width, (t + 1) * width) for t in range(3))
    mb = low(merged[...])
    big[0] = mb
    mid, slope = gelu_pair(nt(mb, adn[...]))
    proj[:, mid_at], proj[:, slope_at] = low(mid), low(slope)
    proj[:, ku_at] = low(nn(big[0], wmat[...]) + shift[...])
    sc = jnp.where(live, nn(proj[:, mid_at] * proj[:, ku_at], gather_mat) * factor, NEG)
    e = jnp.exp(sc - jnp.max(sc, axis=1, keepdims=True))
    jprob[...] = e * (1.0 / jnp.sum(e, axis=1, keepdims=True))
    big[1] = low(nt(low(jprob[...]), gather_mat)) * proj[:, mid_at]
    big[1] = low(merged[...] + nn(big[1], aup[...]))
    merged[...] += nt(big[1], vmat[...])
    out_copies = []
    for b in range(rows // seq_len):
        rs = pl.ds(b * seq_len, seq_len)
        n2, r2 = normalize(merged[rs, :])
        if b >= 2:
            out_copies[b - 2].wait()
        stage[b % 2] = n2 * gain2
        out_copies.append(mv.local(stage.at[b % 2], layer_out.at[rs]))
        gc = norm_back(n2, r2, ct[rs, :].astype(F32) * gain2)
        merged[rs, :] = gc
        big[2, rs, :] = low(gc)
    gm = nn(big[2], vmat[...])
    merged[...] += gm
    big[3] = low(gm)
    big[3] = low(nt(big[3], aup[...]))
    gp = nn(proj[:, mid_at] * big[3], gather_mat)
    jp = jprob[...]
    gs = low(jp * (gp - jnp.sum(jp * gp, axis=1, keepdims=True)) * factor)
    for b in range(rows // block):
        rs = pl.ds(b * block, block)
        at = slice(b * block, (b + 1) * block)
        gs_wide = nt(gs[at], gather_mat)
        jp_wide = nt(low(jp[at]), gather_mat)
        slope = proj[rs, slope_at].astype(F32)
        g_pre = slope * (jp_wide * big[3, rs, :].astype(F32) + gs_wide * proj[rs, ku_at].astype(F32))
        proj[rs, mid_at] = low(gs_wide) * proj[rs, mid_at]
        proj[rs, slope_at] = low(g_pre)
    merged[...] += nt(proj[:, mid_at], wmat[...]) + nn(proj[:, slope_at], adn[...])
    for copy in out_copies[-2:]:
        copy.wait()

    zt = proj[:, mid_at]
    small = jnp.sum(zt.astype(F32), axis=0, keepdims=True)
    vmat[...] = low(tn(big[2], big[1]))
    rb = low(tn(zt, big[0]))
    wmat[...] = low(nn(mmat[...], rb))
    inner = low(nt(rb, qmat[...]))
    qmat[...] = low(tn(inner, aup[...]))
    tail = jnp.concatenate((small, jnp.zeros((PLANE - 3 * share - 1, width), F32)), axis=0)

    def lay(i, carry):
        at = pl.ds(pl.multiple_of(i * piece, piece), piece)
        mats = [mat[at, :].astype(F32) for mat in (wmat, qmat, vmat)]
        for k in range(parts):
            jbuf[i // 4, lax.rem(i // 2, 2), lax.rem(i, 2), k] = low(
                jnp.concatenate([m[k * share : (k + 1) * share] for m in mats] + [tail], axis=0)
            )
        return carry

    lax.fori_loop(0, 8, lay, 0)

    lo, hi = pl.ds(0, parts // 2), pl.ds(parts // 2, parts // 2)

    def add(dst, src):
        dst[...] = low(dst[...].astype(F32) + src[...].astype(F32))

    s_core = mv.remote(jbuf.at[:, :, 1 - c], rc, cn)
    probs_back = mv.local(probs_out, big)
    proj_back = mv.local(proj_out, proj)

    ct[...] = low(merged[...])
    for j in range(parts):
        back[j] = low(nt(ct[...], wd[j]) * back[j].astype(F32))
        if j == 1:
            s_core.wait_recv()
            for yy in range(2):
                for xx in range(2):
                    add(jbuf.at[yy, xx, c], rc.at[yy, xx])
            s_xa = mv.remote(jbuf.at[:, 1 - x, c, lo], rxa, xn)
            s_yb = mv.remote(jbuf.at[1 - y, :, c, hi], ryb, yn)
    for b in range(rows // block):
        rs = pl.ds(b * block, block)
        total = merged[rs, :]
        for j in range(parts):
            total += nt(back[j, rs, :], wu[j])
        g_sum = norm_back(n1[rs, :].astype(F32), r1[rs, :], total * gain1)
        merged[rs, :] = g_sum
        back[0, rs, :] = low(nt(low(g_sum), w_out))
    s_xa.wait_recv()
    s_yb.wait_recv()
    for i in range(2):
        add(jbuf.at[i, x, c, lo], rxa.at[i])
        add(jbuf.at[y, i, c, hi], ryb.at[i])
    s_ya = mv.remote(jbuf.at[1 - y, x, c, lo], rya, yn)
    s_xb = mv.remote(jbuf.at[y, 1 - x, c, hi], rxb, xn)
    probs_back.wait()
    proj_back.wait()

    s_z = []
    for s in range(seqs):
        rs = pl.ds(s * seq_len, seq_len)

        def one_back(hp, carry, s=s, rs=rs):
            qp, kp, vp = (proj[rs, at_pair(hp, t)] for t in range(3))
            go = back[0, rs, at_pair(hp, 0)]
            both = go.astype(F32) * ctx[rs, at_pair(hp, 0)].astype(F32)
            gq = gk = gv = None
            for h in range(2):
                mask, mask_s = half_mask(h, 1.0), half_mask(h, scale)
                pb = big[prob_ref(s, hp, h)]
                delta = jnp.sum(both * mask.astype(F32), axis=1, keepdims=True)
                ds = low(pb.astype(F32) * (nt(go, vp * mask) - delta))
                terms = nn(ds, kp * mask_s), tn(ds, qp * mask_s), tn(pb, go * mask)
                gq, gk, gv = terms if gq is None else (gq + terms[0], gk + terms[1], gv + terms[2])
            for t, g in enumerate((gq, gk, gv)):
                proj[rs, at_pair(hp, t)] = low(g)
            return carry

        lax.fori_loop(0, pairs, one_back, 0, unroll=6)
        if s == 1:
            s_ya.wait_recv()
            s_xb.wait_recv()
            add(jbuf.at[y, x, c, lo], rya)
            add(jbuf.at[y, x, c, hi], rxb)
            for k in range(1, parts):
                s_z.append(
                    mv.remote(jbuf.at[y, x, c, lax.rem(z + k, parts)], rz.at[k - 1], zn[k])
                )
        if s % 2 == 1:
            b = s // 2
            rs = pl.ds(b * block, block)
            total = merged[rs, :]
            for t in range(3):
                total += nn(proj[rs, t * width : (t + 1) * width], wq[t].reshape(width, width))
            merged[rs, :] = total
            s_z.append(mv.local(merged.at[rs], grad_out.at[rs]))

    total = jbuf[y, x, c, z].astype(F32)
    for k in range(1, parts):
        s_z[k - 1].wait_recv()
        total += rz[k - 1].astype(F32)
    flow = total[3 * share : 3 * share + 8]
    turned = nn(low(flow), aup[...])
    key_part = total[share : 2 * share] + bias_col * turned[0:1]
    g_bias = jnp.sum(own_m[...] * flow[0:1], axis=1, keepdims=True)
    join_out[0:share, :] = total[0:share]
    join_out[share : 2 * share, :] = key_part
    join_out[2 * share : 3 * share, :] = total[2 * share : 3 * share]
    join_out[3 * share : 4 * share, :] = jnp.broadcast_to(g_bias, (share, width))
    mv.drain()
    for copy in s_z[parts - 1 :]:
        copy.wait()


def local(
    tokens,
    segment_ids,
    row_ends,
    type_rows,
    ln1_gain,
    attn_qkv,
    attn_out,
    ffn_up,
    ffn_down,
    adapter_down,
    adapter_up,
    ln2_gain,
    joining_query,
    joining_key,
    joining_value,
    query_bias,
    cotangent,
):
    dp, parts = lax.axis_size("dp"), lax.axis_size("mp")
    dpi, z = lax.axis_index("dp"), lax.axis_index("mp")
    rows, width = tokens.shape
    seqs = row_ends.shape[0] // parts
    seq_len = rows // seqs
    adapters, _, bottle = adapter_down.shape
    share = width // (8 * parts)
    axes = ("dp", "mp")

    joins = (joining_query, joining_key, joining_value)
    bias = query_bias
    if dp > 8:
        at = (lax.rem(dpi, 8) * parts + z) * share
        joins = tuple(
            lax.dynamic_slice_in_dim(lax.all_gather(m, axes, axis=1, tiled=True), at, share, 1)
            for m in joins
        )
        bias = lax.dynamic_slice_in_dim(lax.all_gather(bias, axes, axis=0, tiled=True), at, share, 0)
    qkv_in = jnp.transpose(attn_qkv, (0, 2, 1))

    cols = attn_qkv.shape[2]
    ff = ffn_up.shape[1]
    dims = (rows, width, seqs, seq_len, parts, adapters, bottle, share)
    mat = pltpu.VMEM((width, width), BF)
    any_, vm = pl.BlockSpec(memory_space=pl.ANY), pl.BlockSpec(memory_space=pltpu.VMEM)
    sm = pl.BlockSpec(memory_space=pltpu.SMEM)
    planes = lambda *lead: pltpu.VMEM(lead + (PLANE, width), BF)
    out = pl.pallas_call(
        functools.partial(kernel, dims),
        out_shape=(
            jax.ShapeDtypeStruct((rows, width), F32),
            jax.ShapeDtypeStruct((rows, width), F32),
            jax.ShapeDtypeStruct((4 * share, width), F32),
            jax.ShapeDtypeStruct((parts, rows, width), BF),
            jax.ShapeDtypeStruct((rows, 3 * width), BF),
        ),
        in_specs=[any_, any_, vm, sm, vm, vm, vm, vm, any_, any_, any_, any_, any_, any_, vm, vm, vm],
        out_specs=(any_, any_, vm, any_, any_),
        scratch_shapes=[
            pltpu.VMEM((3, parts, cols, width), BF),
            pltpu.VMEM((parts, cols, width), BF),
            pltpu.VMEM((parts, width, ff), BF),
            pltpu.VMEM((parts, ff, width), BF),
            mat, mat, mat, mat, mat, mat,
            pltpu.VMEM((1, width), F32),
            planes(2, 2, 2, parts),
            planes(2, 2, parts),
            planes(2, parts // 2),
            planes(2, parts // 2),
            planes(parts // 2),
            planes(parts // 2),
            planes(parts - 1),
            pltpu.VMEM((rows, width), BF),
            pltpu.VMEM((rows, 3 * width), BF),
            pltpu.VMEM((parts, rows, ff), BF),
            pltpu.VMEM((parts, rows, ff), BF),
            pltpu.VMEM((rows, width), BF),
            pltpu.VMEM((rows, width), BF),
            pltpu.VMEM((rows, 1), F32),
            pltpu.VMEM((rows, width), F32),
            pltpu.VMEM((2, seq_len, width), F32),
            pltpu.VMEM((rows, 128), F32),
            pltpu.VMEM((share, width), F32),
            pltpu.SemaphoreType.DMA((160,)),
            pltpu.SemaphoreType.DMA((160,)),
        ],
        compiler_params=pltpu.CompilerParams(
            collective_id=0, has_side_effects=True, vmem_limit_bytes=VMEM_LIMIT
        ),
    )(
        tokens, cotangent, segment_ids.reshape(-1, 128), row_ends, type_rows,
        ln1_gain.reshape(-1, 128), ln2_gain.reshape(-1, 128), bias[None, :], qkv_in, attn_out, ffn_up, ffn_down,
        jnp.transpose(adapter_down, (0, 2, 1)).reshape(adapters * bottle, width),
        adapter_up.reshape(adapters * bottle, width), *(jnp.transpose(m) for m in joins),
    )
    layer_out, g_in, grads, _, _ = out
    if dp > 8:
        at = (lax.rem(dpi, 8) * parts + z) * share
        own = width // (dp * parts)
        full = jnp.zeros((4, width, width), F32)
        full = lax.dynamic_update_slice_in_dim(full, grads.reshape(4, share, width), at, 1)
        full = lax.psum(full, axes)
        grads = lax.dynamic_slice_in_dim(full, (dpi * parts + z) * own, own, 1)
    else:
        grads = grads.reshape(4, share, width)
    g_q, g_k, g_v = (jnp.transpose(grads[i]) for i in range(3))
    return (layer_out, g_in, g_q, g_k, g_v, grads[3, :, 0])


VMEM_LIMIT = 63 * 1024 * 1024


def solution(mesh):
    in_specs = (
        P(("dp", "mp"), None),
        P("dp"),
        P("dp"),
        P(),
        P(),
        P(None, None, "mp"),
        P("mp", None),
        P(None, "mp"),
        P("mp", None),
        P(),
        P(),
        P(),
        P(None, ("dp", "mp")),
        P(None, ("dp", "mp")),
        P(None, ("dp", "mp")),
        P(("dp", "mp")),
        P(("dp", "mp"), None),
    )
    out_specs = (
        P(("dp", "mp"), None),
        P(("dp", "mp"), None),
        P(None, ("dp", "mp")),
        P(None, ("dp", "mp")),
        P(None, ("dp", "mp")),
        P(("dp", "mp")),
    )
    return jax.shard_map(local, mesh=mesh, in_specs=in_specs, out_specs=out_specs, check_vma=False)
```

```python
import functools

import jax
import jax.numpy as jnp
from jax import lax
from jax.experimental import pallas as pl
from jax.experimental.pallas import tpu as pltpu
from jax.sharding import PartitionSpec as P

HEAD = 64
EPS = 1e-06
ROOT_HALF = 0.7071067811865476
INV_ROOT_2PI = 0.3989422804014327
NEG = -1e30
MESH = pl.DeviceIdType.MESH
PLANE = 80
BF = jnp.bfloat16
F32 = jnp.float32


def nn(a, b):
    return jnp.dot(a, b, preferred_element_type=F32)


def nt(a, b):
    return lax.dot_general(a, b, (((1,), (1,)), ((), ())), preferred_element_type=F32)


def tn(a, b):
    return lax.dot_general(a, b, (((0,), (0,)), ((), ())), preferred_element_type=F32)


def low(v):
    return v.astype(BF)


def gelu_pair(v):
    cdf = 0.5 + 0.5 * lax.erf(v * ROOT_HALF)
    return v * cdf, cdf + v * (INV_ROOT_2PI * jnp.exp(-0.5 * (v * v)))


def mean(v):
    return jnp.sum(v, axis=-1, keepdims=True) * (1.0 / v.shape[-1])


def normalize(v):
    center = v - mean(v)
    r = lax.rsqrt(mean(center * center) + EPS)
    return center * r, r


def norm_back(n, r, t):
    return r * (t - mean(t) - n * mean(t * n))


def half_mask(h, value):
    lane = lax.broadcasted_iota(jnp.int32, (1, 2 * HEAD), 1)
    inside = (lane >= h * HEAD) & (lane < (h + 1) * HEAD)
    return jnp.where(inside, jnp.asarray(value, F32), jnp.asarray(0.0, F32)).astype(BF)


def flat_row(ref):
    return jnp.concatenate([ref[i : i + 1, :] for i in range(ref.shape[0])], axis=1)


class Mover:
    def __init__(self, send, recv):
        self.send, self.recv, self.count, self.open = send, recv, 0, []

    def slot(self):
        self.count += 1
        return self.count - 1

    def remote(self, src, dst, peer, start=True):
        i = self.slot()
        copy = pltpu.make_async_remote_copy(
            src_ref=src, dst_ref=dst, send_sem=self.send.at[i], recv_sem=self.recv.at[i],
            device_id=peer, device_id_type=MESH,
        )
        copy.start()
        self.open.append(copy)
        return copy

    def local(self, src, dst):
        copy = pltpu.make_async_copy(src, dst, self.send.at[self.slot()])
        copy.start()
        return copy

    def drain(self):
        for copy in self.open:
            copy.wait_send()
        self.open = []


def kernel(
    dims,
    tok_in, cot_in, seg_in, ends_in, type_in, gain1_in, gain2_in, bias_in, qkv_in, out_in, up_in, down_in, adn_in, aup_in, jq_in, jk_in, jv_in,
    layer_out, grad_out, join_out, bias_out, probs_out, proj_out,
    wq, wo, wu, wd, aup, adn, wmat, mmat, qmat, vmat, shift, jbuf,
    rc, rxa, ryb, rya, rxb, rz,
    ct, proj, big, back, ctx, n1, r1, merged, stage, jprob, own_m,
    send, recv,
):
    rows, width, seqs, seq_len, parts, adapters, bottle, share = dims
    d, z = lax.axis_index("dp"), lax.axis_index("mp")
    p = lax.rem(d, 8)
    c, x, y = lax.rem(p, 2), lax.rem(p // 2, 2), p // 4
    xn = (d + 2 - 4 * x, z)
    yn = (d + 4 - 8 * y, z)
    cn = (d + 1 - 2 * c, z)
    zn = [None] + [(d, lax.rem(z + k, parts)) for k in range(1, parts)]
    q = p // 2
    qx, qy = q + 1 - 2 * x, q + 2 - 4 * y
    qd = qx + 2 - 4 * y
    factor = width ** (-0.5)
    half = width // 2

    barrier = pltpu.get_barrier_semaphore()
    for peer in [xn, yn, cn] + zn[1:]:
        pl.semaphore_signal(barrier, inc=1, device_id=peer, device_id_type=MESH)
    pl.semaphore_wait(barrier, 2 + parts)

    mv = Mover(send, recv)

    class Unit:
        def __init__(self, src, dst, piece, split, needs):
            self.src, self.dst, self.piece, self.split, self.needs = src, dst, piece, split, needs
            self.z, self.x, self.y, self.dx, self.dy, self.cc = {}, {}, {}, {}, {}, {}

        def ask(self, *steps):
            for r in steps:
                self.z[r] = mv.remote(self.src, self.dst(parts - r), zn[parts - r])

        def first(self, g):
            for k in self.needs[g]:
                self.z[k].wait_recv()
            ref = self.piece(g, q, c, 0, None)
            self.x[g] = mv.remote(ref, ref, xn)
            self.y[g] = mv.remote(ref, ref, yn)
            self.cc[g, 0] = mv.remote(ref, ref, cn)

        def second(self, g):
            self.x[g].wait_recv()
            part = self.split(0, g)
            if part is not None:
                ref = self.piece(g, qx, c, *part)
                self.dy[g] = mv.remote(ref, ref, yn)
            ref = self.piece(g, qx, c, 0, None)
            self.cc[g, 1] = mv.remote(ref, ref, cn)
            self.y[g].wait_recv()
            part = self.split(1, g)
            if part is not None:
                ref = self.piece(g, qy, c, *part)
                self.dx[g] = mv.remote(ref, ref, xn)
            ref = self.piece(g, qy, c, 0, None)
            self.cc[g, 2] = mv.remote(ref, ref, cn)

        def third(self, g):
            for got in (self.dx, self.dy):
                if g in got:
                    got[g].wait_recv()
            ref = self.piece(g, qd, c, 0, None)
            self.cc[g, 3] = mv.remote(ref, ref, cn)

        def last(self, g):
            for k in range(4):
                self.cc[g, k].wait_recv()

    def frozen(src, buf, piece_rows, cut, groups, lead):
        def window(ref, zs, chip, core, off, count):
            count = piece_rows if count is None else count
            at = (zs, pl.ds(chip * piece_rows + off, count), pl.ds(pl.multiple_of(core * half, half), half))
            return ref.at[(slice(None),) * lead + at]

        def own():
            at = (pl.ds(q * piece_rows, piece_rows), pl.ds(pl.multiple_of(c * half, half), half))
            return src.at[(slice(None),) * lead + at]

        return Unit(
            own(),
            lambda k: window(buf, parts - k, q, c, 0, None),
            lambda g, chip, core, off, count: window(buf, groups[g], chip, core, off, count),
            lambda which, g: ((0, cut), (cut, piece_rows - cut))[which],
            {g: (g,) if g else range(1, parts) for g in groups},
        )

    heads_rows = wo.shape[1]
    near = (3, 1, 2)
    each = {r: pl.ds(r, 1) for r in near}
    whole = {0: pl.ds(1, parts - 1)}
    u_qkv = frozen(qkv_in, wq, heads_rows // 4, 32, each, 1)
    u_out = frozen(out_in, wo, heads_rows // 4, 16, whole, 0)
    u_up = frozen(up_in, wu, wu.shape[1] // 4, wu.shape[1] // 8, each, 0)
    u_down = frozen(down_in, wd, wd.shape[1] // 4, wd.shape[1] // 8, each, 0)

    def jpiece(g, chip, core, off, count):
        ref = jbuf.at[chip // 2, lax.rem(chip, 2), core, lax.rem(z + g, parts)]
        return ref if count is None else ref.at[pl.ds(off, count)]

    u_join = Unit(
        jbuf.at[y, x, c, z],
        lambda k: jbuf.at[y, x, c, z],
        jpiece,
        lambda which, g: ((0, 48), (48, PLANE - 48))[which],
        {0: (), 1: (1,), 2: (2,), 3: (3,)},
    )

    u_qkv.ask(3, 1)
    l_up = mv.local(aup_in, aup)
    l_dn = mv.local(adn_in, adn)
    l_qkv = mv.local(qkv_in, wq.at[:, 0])
    l_tok = mv.local(tok_in, ct)
    l_out = mv.local(out_in, wo.at[0])
    l_wu = mv.local(up_in, wu.at[0])
    l_wd = mv.local(down_in, wd.at[0])

    gain1, gain2 = flat_row(gain1_in), flat_row(gain2_in)
    spot = lax.broadcasted_iota(jnp.int32, (share, share), 0) == lax.broadcasted_iota(
        jnp.int32, (share, share), 1
    )
    bias_col = jnp.sum(jnp.where(spot, bias_in[...].astype(F32), 0.0), axis=1, keepdims=True)
    l_up.wait()
    m_low = low(nt(jk_in[...], aup[...])).astype(F32)
    own_m[...] = m_low
    part_shift = jnp.sum(bias_col * m_low, axis=0, keepdims=True)
    high = low(part_shift).astype(F32)
    blank = jnp.zeros((PLANE - 3 * share - 2, width), F32)
    tail = jnp.concatenate((high, part_shift - high, blank), axis=0)
    jbuf[y, x, c, z] = low(
        jnp.concatenate((jq_in[...].astype(F32), m_low, jv_in[...].astype(F32), tail), axis=0)
    )
    u_join.first(0)
    u_qkv.first(3)
    u_qkv.first(1)
    u_qkv.ask(2)
    u_out.ask(3, 1, 2)
    u_join.second(0)
    u_qkv.second(3)
    u_qkv.first(2)
    u_up.ask(3, 1)
    u_qkv.second(1)
    u_join.third(0)
    u_out.first(0)
    u_up.ask(2)
    u_qkv.third(3)
    u_qkv.second(2)
    u_qkv.third(1)
    u_up.first(3)
    u_up.first(1)
    u_down.ask(3, 1)
    u_out.second(0)
    u_qkv.third(2)
    for r in near:
        u_qkv.last(r)

    l_tok.wait()
    l_qkv.wait()
    chunks = rows // 128
    seg = seg_in[pl.ds(pl.multiple_of(z * chunks, chunks), chunks), :].astype(F32)
    column = jnp.transpose(seg)
    per_seq = seq_len // 128
    type_f = type_in[...].astype(F32)

    def summed(s):
        rs = pl.ds(s * seq_len, seq_len)
        picks = [column[:, k : k + 1] for k in range(s * per_seq, (s + 1) * per_seq)]
        pick = jnp.concatenate(picks, axis=0) > 0.5
        return ct[rs, :].astype(F32) + jnp.where(pick, type_f[1:2], type_f[0:1])

    xb = jnp.concatenate([low(summed(s)) for s in range(seqs)], axis=0)
    for t in range(3):
        proj[:, t * width : (t + 1) * width] = low(nt(xb, wq[t].reshape(width, width)))
        if t == 0:
            u_out.third(0)
            u_up.first(2)
            u_down.ask(2)
        if t == 1:
            u_up.second(3)
    u_up.second(1)

    pairs = width // (2 * HEAD)
    scale = HEAD ** (-0.5)
    probs_copies = []

    def at_pair(hp, t):
        return pl.ds(pl.multiple_of(t * width + hp * 2 * HEAD, 2 * HEAD), 2 * HEAD)

    def prob_ref(s, hp, h):
        head = hp * 2 + h
        per = width // seq_len
        return (
            head // per,
            pl.ds(s * seq_len, seq_len),
            pl.ds(pl.multiple_of(lax.rem(head, per) * seq_len, seq_len), seq_len),
        )

    places = lax.broadcasted_iota(jnp.int32, (1, seq_len), 1)
    for s in range(seqs):
        rs = pl.ds(s * seq_len, seq_len)
        hidden = jnp.where(places <= ends_in[z * seqs + s], 0.0, NEG)

        def one(hp, carry, s=s, rs=rs, hidden=hidden):
            qp, kp, vp = (proj[rs, at_pair(hp, t)] for t in range(3))
            total = None
            for h in range(2):
                sc = nt(qp, kp * half_mask(h, scale)) + hidden
                e = jnp.exp(sc - jnp.max(sc, axis=1, keepdims=True))
                pb = low(e * (1.0 / jnp.sum(e, axis=1, keepdims=True)))
                big[prob_ref(s, hp, h)] = pb
                term = nn(pb, vp * half_mask(h, 1.0))
                total = term if total is None else total + term
            ctx[rs, at_pair(hp, 0)] = low(total)
            return carry

        lax.fori_loop(0, pairs, one, 0, unroll=3)
        probs_copies.append(mv.local(big.at[:, rs], probs_out.at[:, rs]))
        if s == 0:
            u_up.third(3)
            u_down.first(3)
            u_down.first(1)
            u_join.ask(3, 1)
        if s == 1:
            u_up.second(2)
            u_up.third(1)
            u_down.first(2)
            u_join.ask(2)
        if s == 2:
            u_down.second(3)
            u_up.third(2)
            u_out.last(0)
        if s == 3:
            u_down.second(1)
            u_join.first(3)
            u_join.first(1)
    proj_copy = mv.local(proj, proj_out)

    l_out.wait()
    block = 2 * seq_len
    w_out = wo[...].reshape(width, width)
    for b in range(rows // block):
        rs = pl.ds(b * block, block)
        xs = jnp.concatenate((summed(2 * b), summed(2 * b + 1)), axis=0)
        n, r = normalize(xs + nn(ctx[rs, :], w_out))
        n1[rs, :] = low(n)
        r1[rs, :] = r
        h = n * gain1
        merged[rs, :] = h
        ct[rs, :] = low(h)
    for copy in probs_copies:
        copy.wait()

    l_wu.wait()
    for i, j in enumerate((0,) + near):
        if i == 0:
            u_down.third(3)
            u_join.first(2)
        else:
            u_up.last(j)
        act, slope = gelu_pair(nn(ct[...], wu[j]))
        big[j] = low(act)
        back[j] = low(slope)
        if i == 1:
            u_down.second(2)
            u_down.third(1)
        if i == 2:
            u_join.second(3)
    l_cot = mv.local(cot_in, ct)
    l_wd.wait()
    for i, j in enumerate((0,) + near):
        if i == 1:
            u_down.third(2)
            u_join.second(1)
        if i == 3:
            u_join.third(3)
        if i > 0:
            u_down.last(j)
        merged[...] += nn(big[j], wd[j])
    u_join.third(1)
    u_join.second(2)
    l_dn.wait()
    proj_copy.wait()
    mid_at, slope_at, ku_at = (slice(t * width, (t + 1) * width) for t in range(3))
    mb = low(merged[...])
    big[0] = mb
    mid, slope = gelu_pair(nt(mb, adn[...]))
    proj[:, mid_at], proj[:, slope_at] = low(mid), low(slope)
    u_join.third(2)
    for r in (0,) + near:
        u_join.last(r)

    piece = parts * share

    def pack(i, total):
        planes = [jbuf[i // 4, lax.rem(i // 2, 2), lax.rem(i, 2), k].astype(F32) for k in range(parts)]
        at = pl.ds(pl.multiple_of(i * piece, piece), piece)
        for n, mat in enumerate((qmat, mmat, vmat)):
            mat[at, :] = low(
                jnp.concatenate([pl_[n * share : (n + 1) * share] for pl_ in planes], axis=0)
            )
        for pl_ in planes:
            total += pl_[3 * share : 3 * share + 1] + pl_[3 * share + 1 : 3 * share + 2]
        return total

    shift[...] = lax.fori_loop(0, 8, pack, jnp.zeros((1, width), F32))
    wmat[...] = low(tn(qmat[...], mmat[...]))
    mv.drain()

    units = adapters * bottle
    row_i = lax.broadcasted_iota(jnp.int32, (units, 128), 0)
    lane_i = lax.broadcasted_iota(jnp.int32, (units, 128), 1)
    gather_mat = low(
        jnp.where((row_i >= lane_i * bottle) & (row_i < (lane_i + 1) * bottle), 1.0, 0.0)
    )
    live = lax.broadcasted_iota(jnp.int32, (1, 128), 1) < adapters
    l_cot.wait()
    proj[:, ku_at] = low(nn(big[0], wmat[...]) + shift[...])
    sc = jnp.where(live, nn(proj[:, mid_at] * proj[:, ku_at], gather_mat) * factor, NEG)
    e = jnp.exp(sc - jnp.max(sc, axis=1, keepdims=True))
    jprob[...] = e * (1.0 / jnp.sum(e, axis=1, keepdims=True))
    big[1] = low(nt(low(jprob[...]), gather_mat)) * proj[:, mid_at]
    big[1] = low(merged[...] + nn(big[1], aup[...]))
    merged[...] += nt(big[1], vmat[...])
    out_copies = []
    for b in range(rows // seq_len):
        rs = pl.ds(b * seq_len, seq_len)
        n2, r2 = normalize(merged[rs, :])
        if b >= 2:
            out_copies[b - 2].wait()
        stage[b % 2] = n2 * gain2
        out_copies.append(mv.local(stage.at[b % 2], layer_out.at[rs]))
        gc = norm_back(n2, r2, ct[rs, :].astype(F32) * gain2)
        merged[rs, :] = gc
        big[2, rs, :] = low(gc)
    gm = nn(big[2], vmat[...])
    merged[...] += gm
    big[3] = low(gm)
    big[3] = low(nt(big[3], aup[...]))
    gp = nn(proj[:, mid_at] * big[3], gather_mat)
    jp = jprob[...]
    gs = low(jp * (gp - jnp.sum(jp * gp, axis=1, keepdims=True)) * factor)
    for b in range(rows // block):
        rs = pl.ds(b * block, block)
        at = slice(b * block, (b + 1) * block)
        gs_wide = nt(gs[at], gather_mat)
        jp_wide = nt(low(jp[at]), gather_mat)
        slope = proj[rs, slope_at].astype(F32)
        g_pre = slope * (jp_wide * big[3, rs, :].astype(F32) + gs_wide * proj[rs, ku_at].astype(F32))
        proj[rs, mid_at] = low(gs_wide) * proj[rs, mid_at]
        proj[rs, slope_at] = low(g_pre)
    merged[...] += nt(proj[:, mid_at], wmat[...]) + nn(proj[:, slope_at], adn[...])
    for copy in out_copies[-2:]:
        copy.wait()

    zt = proj[:, mid_at]
    small = jnp.sum(zt.astype(F32), axis=0, keepdims=True)
    vmat[...] = low(tn(big[2], big[1]))
    rb = low(tn(zt, big[0]))
    wmat[...] = low(nn(mmat[...], rb))
    inner = low(nt(rb, qmat[...]))
    qmat[...] = low(tn(inner, aup[...]))
    tail = jnp.concatenate((small, jnp.zeros((PLANE - 3 * share - 1, width), F32)), axis=0)

    def lay(i, carry):
        at = pl.ds(pl.multiple_of(i * piece, piece), piece)
        mats = [mat[at, :].astype(F32) for mat in (wmat, qmat, vmat)]
        for k in range(parts):
            jbuf[i // 4, lax.rem(i // 2, 2), lax.rem(i, 2), k] = low(
                jnp.concatenate([m[k * share : (k + 1) * share] for m in mats] + [tail], axis=0)
            )
        return carry

    lax.fori_loop(0, 8, lay, 0)

    lo, hi = pl.ds(0, parts // 2), pl.ds(parts // 2, parts // 2)

    def add(dst, src):
        dst[...] = low(dst[...].astype(F32) + src[...].astype(F32))

    s_core = mv.remote(jbuf.at[:, :, 1 - c], rc, cn)
    probs_back = mv.local(probs_out, big)
    proj_back = mv.local(proj_out, proj)

    ct[...] = low(merged[...])
    for j in range(parts):
        back[j] = low(nt(ct[...], wd[j]) * back[j].astype(F32))
        if j == 1:
            s_core.wait_recv()
            for yy in range(2):
                for xx in range(2):
                    add(jbuf.at[yy, xx, c], rc.at[yy, xx])
            s_xa = mv.remote(jbuf.at[:, 1 - x, c, lo], rxa, xn)
            s_yb = mv.remote(jbuf.at[1 - y, :, c, hi], ryb, yn)
    for b in range(rows // block):
        rs = pl.ds(b * block, block)
        total = merged[rs, :]
        for j in range(parts):
            total += nt(back[j, rs, :], wu[j])
        g_sum = norm_back(n1[rs, :].astype(F32), r1[rs, :], total * gain1)
        merged[rs, :] = g_sum
        back[0, rs, :] = low(nt(low(g_sum), w_out))
    s_xa.wait_recv()
    s_yb.wait_recv()
    for i in range(2):
        add(jbuf.at[i, x, c, lo], rxa.at[i])
        add(jbuf.at[y, i, c, hi], ryb.at[i])
    s_ya = mv.remote(jbuf.at[1 - y, x, c, lo], rya, yn)
    s_xb = mv.remote(jbuf.at[y, 1 - x, c, hi], rxb, xn)
    probs_back.wait()
    proj_back.wait()

    s_z = []
    for s in range(seqs):
        rs = pl.ds(s * seq_len, seq_len)

        def one_back(hp, carry, s=s, rs=rs):
            qp, kp, vp = (proj[rs, at_pair(hp, t)] for t in range(3))
            go = back[0, rs, at_pair(hp, 0)]
            both = go.astype(F32) * ctx[rs, at_pair(hp, 0)].astype(F32)
            gq = gk = gv = None
            for h in range(2):
                mask, mask_s = half_mask(h, 1.0), half_mask(h, scale)
                pb = big[prob_ref(s, hp, h)]
                delta = jnp.sum(both * mask.astype(F32), axis=1, keepdims=True)
                ds = low(pb.astype(F32) * (nt(go, vp * mask) - delta))
                terms = nn(ds, kp * mask_s), tn(ds, qp * mask_s), tn(pb, go * mask)
                gq, gk, gv = terms if gq is None else (gq + terms[0], gk + terms[1], gv + terms[2])
            for t, g in enumerate((gq, gk, gv)):
                proj[rs, at_pair(hp, t)] = low(g)
            return carry

        lax.fori_loop(0, pairs, one_back, 0, unroll=6)
        if s == 1:
            s_ya.wait_recv()
            s_xb.wait_recv()
            add(jbuf.at[y, x, c, lo], rya)
            add(jbuf.at[y, x, c, hi], rxb)
            for k in range(1, parts):
                s_z.append(
                    mv.remote(jbuf.at[y, x, c, lax.rem(z + k, parts)], rz.at[k - 1], zn[k])
                )
        if s % 2 == 1:
            b = s // 2
            rs = pl.ds(b * block, block)
            total = merged[rs, :]
            for t in range(3):
                total += nn(proj[rs, t * width : (t + 1) * width], wq[t].reshape(width, width))
            merged[rs, :] = total
            s_z.append(mv.local(merged.at[rs], grad_out.at[rs]))

    total = jbuf[y, x, c, z].astype(F32)
    for k in range(1, parts):
        s_z[k - 1].wait_recv()
        total += rz[k - 1].astype(F32)
    flow = total[3 * share : 3 * share + 8]
    turned = nn(low(flow), aup[...])
    key_part = total[share : 2 * share] + bias_col * turned[0:1]
    g_bias = jnp.sum(own_m[...] * flow[0:1], axis=1, keepdims=True)
    join_out[0:share, :] = total[0:share]
    join_out[share : 2 * share, :] = key_part
    join_out[2 * share : 3 * share, :] = total[2 * share : 3 * share]
    wide = jnp.where(
        lax.broadcasted_iota(jnp.int32, (share, 128), 0)
        == lax.broadcasted_iota(jnp.int32, (share, 128), 1),
        g_bias,
        0.0,
    )
    bias_out[...] = jnp.broadcast_to(jnp.sum(wide, axis=0, keepdims=True), (8, 128))
    mv.drain()
    for copy in s_z[parts - 1 :]:
        copy.wait()


def hand_over(
    layer_in, grad_in, join_in, bias_in,
    layer_out, grad_out, gq_out, gk_out, gv_out, bias_out,
    held, turned, arrive, leave,
):
    rows, share = layer_in.shape[0] // 4, gq_out.shape[0]
    steps = []
    for n, (src, dst) in enumerate(((layer_in, layer_out), (grad_in, grad_out))):
        for i in range(4):
            at = pl.ds(i * rows, rows)
            steps.append((src.at[at], held.at[n, at], dst.at[at]))
    for i, dst in enumerate((gq_out, gk_out, gv_out)):
        steps.append((join_in.at[pl.ds(i * share, share)], turned.at[i], dst))
    inward = [pltpu.make_async_copy(s, m, arrive.at[i]) for i, (s, m, _) in enumerate(steps)]
    outward = [pltpu.make_async_copy(m, d, leave.at[i]) for i, (_, m, d) in enumerate(steps)]
    for copy in inward:
        copy.start()
    bias_out[...] = bias_in[0:1, 0:share]
    for came, goes in zip(inward, outward):
        came.wait()
        goes.start()
    for copy in outward:
        copy.wait()


def local(
    tokens,
    segment_ids,
    row_ends,
    type_rows,
    ln1_gain,
    attn_qkv,
    attn_out,
    ffn_up,
    ffn_down,
    adapter_down,
    adapter_up,
    ln2_gain,
    joining_query,
    joining_key,
    joining_value,
    query_bias,
    cotangent,
):
    dp, parts = lax.axis_size("dp"), lax.axis_size("mp")
    dpi, z = lax.axis_index("dp"), lax.axis_index("mp")
    rows, width = tokens.shape
    seqs = row_ends.shape[0] // parts
    seq_len = rows // seqs
    adapters, _, bottle = adapter_down.shape
    share = width // (8 * parts)
    axes = ("dp", "mp")

    joins = (joining_query, joining_key, joining_value)
    bias = query_bias
    if dp > 8:
        at = (lax.rem(dpi, 8) * parts + z) * share
        joins = tuple(
            lax.dynamic_slice_in_dim(lax.all_gather(m, axes, axis=1, tiled=True), at, share, 1)
            for m in joins
        )
        bias = lax.dynamic_slice_in_dim(lax.all_gather(bias, axes, axis=0, tiled=True), at, share, 0)
    qkv_in = jnp.transpose(attn_qkv, (0, 2, 1))

    cols = attn_qkv.shape[2]
    ff = ffn_up.shape[1]
    dims = (rows, width, seqs, seq_len, parts, adapters, bottle, share)
    mat = pltpu.VMEM((width, width), BF)
    any_, vm = pl.BlockSpec(memory_space=pl.ANY), pl.BlockSpec(memory_space=pltpu.VMEM)
    sm = pl.BlockSpec(memory_space=pltpu.SMEM)
    planes = lambda *lead: pltpu.VMEM(lead + (PLANE, width), BF)
    out = pl.pallas_call(
        functools.partial(kernel, dims),
        out_shape=(
            jax.ShapeDtypeStruct((rows, width), F32),
            jax.ShapeDtypeStruct((rows, width), F32),
            jax.ShapeDtypeStruct((3 * share, width), F32),
            jax.ShapeDtypeStruct((8, 128), F32),
            jax.ShapeDtypeStruct((parts, rows, width), BF),
            jax.ShapeDtypeStruct((rows, 3 * width), BF),
        ),
        in_specs=[any_, any_, vm, sm, vm, vm, vm, vm, any_, any_, any_, any_, any_, any_, vm, vm, vm],
        out_specs=(any_, any_, vm, vm, any_, any_),
        scratch_shapes=[
            pltpu.VMEM((3, parts, cols, width), BF),
            pltpu.VMEM((parts, cols, width), BF),
            pltpu.VMEM((parts, width, ff), BF),
            pltpu.VMEM((parts, ff, width), BF),
            mat, mat, mat, mat, mat, mat,
            pltpu.VMEM((1, width), F32),
            planes(2, 2, 2, parts),
            planes(2, 2, parts),
            planes(2, parts // 2),
            planes(2, parts // 2),
            planes(parts // 2),
            planes(parts // 2),
            planes(parts - 1),
            pltpu.VMEM((rows, width), BF),
            pltpu.VMEM((rows, 3 * width), BF),
            pltpu.VMEM((parts, rows, ff), BF),
            pltpu.VMEM((parts, rows, ff), BF),
            pltpu.VMEM((rows, width), BF),
            pltpu.VMEM((rows, width), BF),
            pltpu.VMEM((rows, 1), F32),
            pltpu.VMEM((rows, width), F32),
            pltpu.VMEM((2, seq_len, width), F32),
            pltpu.VMEM((rows, 128), F32),
            pltpu.VMEM((share, width), F32),
            pltpu.SemaphoreType.DMA((160,)),
            pltpu.SemaphoreType.DMA((160,)),
        ],
        compiler_params=pltpu.CompilerParams(
            collective_id=0, has_side_effects=True, vmem_limit_bytes=VMEM_LIMIT
        ),
    )(
        tokens, cotangent, segment_ids.reshape(-1, 128), row_ends, type_rows,
        ln1_gain.reshape(-1, 128), ln2_gain.reshape(-1, 128), bias[None, :], qkv_in, attn_out, ffn_up, ffn_down,
        jnp.transpose(adapter_down, (0, 2, 1)).reshape(adapters * bottle, width),
        adapter_up.reshape(adapters * bottle, width), *(jnp.transpose(m) for m in joins),
    )
    layer_out, g_in, grads, g_bias, _, _ = out
    layer_out, g_in, *grads, g_bias = pl.pallas_call(
        hand_over,
        out_shape=tuple(
            jax.ShapeDtypeStruct((n, width), F32) for n in (rows, rows, share, share, share)
        )
        + (jax.ShapeDtypeStruct((1, share), F32),),
        in_specs=[any_] * 3 + [vm],
        out_specs=(any_,) * 5 + (vm,),
        scratch_shapes=[
            pltpu.VMEM((2, rows, width), F32),
            pltpu.VMEM((3, share, width), F32),
            pltpu.SemaphoreType.DMA((11,)),
            pltpu.SemaphoreType.DMA((11,)),
        ],
        compiler_params=pltpu.CompilerParams(vmem_limit_bytes=VMEM_LIMIT),
    )(layer_out, g_in, grads, g_bias)
    g_bias = g_bias[0]
    if dp > 8:
        at = (lax.rem(dpi, 8) * parts + z) * share
        own, first = width // (dp * parts), (dpi * parts + z) * (width // (dp * parts))
        whole = lambda v, axis: lax.psum(
            lax.dynamic_update_slice_in_dim(
                jnp.zeros(v.shape[:axis] + (width,) + v.shape[axis + 1 :], F32), v, at, axis
            ),
            axes,
        )
        grads = lax.dynamic_slice_in_dim(whole(jnp.stack(grads), 1), first, own, 1)
        g_bias = lax.dynamic_slice_in_dim(whole(g_bias, 0), first, own, 0)
    g_q, g_k, g_v = (jnp.transpose(grads[i]) for i in range(3))
    return (layer_out, g_in, g_q, g_k, g_v, g_bias)


VMEM_LIMIT = 63 * 1024 * 1024


def solution(mesh):
    in_specs = (
        P(("dp", "mp"), None),
        P("dp"),
        P("dp"),
        P(),
        P(),
        P(None, None, "mp"),
        P("mp", None),
        P(None, "mp"),
        P("mp", None),
        P(),
        P(),
        P(),
        P(None, ("dp", "mp")),
        P(None, ("dp", "mp")),
        P(None, ("dp", "mp")),
        P(("dp", "mp")),
        P(("dp", "mp"), None),
    )
    out_specs = (
        P(("dp", "mp"), None),
        P(("dp", "mp"), None),
        P(None, ("dp", "mp")),
        P(None, ("dp", "mp")),
        P(None, ("dp", "mp")),
        P(("dp", "mp")),
    )
    return jax.shard_map(local, mesh=mesh, in_specs=in_specs, out_specs=out_specs, check_vma=False)
```

```python
import functools

import jax
import jax.numpy as jnp
from jax import lax
from jax.experimental import pallas as pl
from jax.experimental.pallas import tpu as pltpu
from jax.sharding import PartitionSpec as P

HEAD = 64
EPS = 1e-06
ROOT_HALF = 0.7071067811865476
INV_ROOT_2PI = 0.3989422804014327
NEG = -1e30
MESH = pl.DeviceIdType.MESH
PLANE = 80
BF = jnp.bfloat16
F32 = jnp.float32


def nn(a, b):
    return jnp.dot(a, b, preferred_element_type=F32)


def nt(a, b):
    return lax.dot_general(a, b, (((1,), (1,)), ((), ())), preferred_element_type=F32)


def tn(a, b):
    return lax.dot_general(a, b, (((0,), (0,)), ((), ())), preferred_element_type=F32)


def low(v):
    return v.astype(BF)


def gelu_pair(v):
    cdf = 0.5 + 0.5 * lax.erf(v * ROOT_HALF)
    return v * cdf, cdf + v * (INV_ROOT_2PI * jnp.exp(-0.5 * (v * v)))


def mean(v):
    return jnp.sum(v, axis=-1, keepdims=True) * (1.0 / v.shape[-1])


def normalize(v):
    center = v - mean(v)
    r = lax.rsqrt(mean(center * center) + EPS)
    return center * r, r


def norm_back(n, r, t):
    return r * (t - mean(t) - n * mean(t * n))


def half_mask(h, value):
    lane = lax.broadcasted_iota(jnp.int32, (1, 2 * HEAD), 1)
    inside = (lane >= h * HEAD) & (lane < (h + 1) * HEAD)
    return jnp.where(inside, jnp.asarray(value, F32), jnp.asarray(0.0, F32)).astype(BF)


def flat_row(ref):
    return jnp.concatenate([ref[i : i + 1, :] for i in range(ref.shape[0])], axis=1)


class Mover:
    def __init__(self, send, recv):
        self.send, self.recv, self.count, self.open = send, recv, 0, []

    def slot(self):
        self.count += 1
        return self.count - 1

    def remote(self, src, dst, peer, start=True):
        i = self.slot()
        copy = pltpu.make_async_remote_copy(
            src_ref=src, dst_ref=dst, send_sem=self.send.at[i], recv_sem=self.recv.at[i],
            device_id=peer, device_id_type=MESH,
        )
        copy.start()
        self.open.append(copy)
        return copy

    def local(self, src, dst):
        copy = pltpu.make_async_copy(src, dst, self.send.at[self.slot()])
        copy.start()
        return copy

    def drain(self):
        for copy in self.open:
            copy.wait_send()
        self.open = []


def kernel(
    dims,
    tok_in, cot_in, seg_in, ends_in, type_in, gain1_in, gain2_in, bias_in, qkv_in, out_in, up_in, down_in, adn_in, aup_in, jq_in, jk_in, jv_in,
    layer_out, grad_out, join_out, bias_out, probs_out, proj_out,
    wq, wo, wu, wd, aup, adn, wmat, mmat, qmat, vmat, shift, jbuf,
    rc, rxa, ryb, rya, rxb, rz,
    ct, proj, big, back, ctx, n1, r1, merged, stage, jprob, own_m,
    send, recv,
):
    rows, width, seqs, seq_len, parts, adapters, bottle, share = dims
    d, z = lax.axis_index("dp"), lax.axis_index("mp")
    p = lax.rem(d, 8)
    c, x, y = lax.rem(p, 2), lax.rem(p // 2, 2), p // 4
    xn = (d + 2 - 4 * x, z)
    yn = (d + 4 - 8 * y, z)
    cn = (d + 1 - 2 * c, z)
    zn = [None] + [(d, lax.rem(z + k, parts)) for k in range(1, parts)]
    q = p // 2
    qx, qy = q + 1 - 2 * x, q + 2 - 4 * y
    qd = qx + 2 - 4 * y
    factor = width ** (-0.5)
    half = width // 2

    barrier = pltpu.get_barrier_semaphore()
    for peer in [xn, yn, cn] + zn[1:]:
        pl.semaphore_signal(barrier, inc=1, device_id=peer, device_id_type=MESH)
    pl.semaphore_wait(barrier, 2 + parts)

    mv = Mover(send, recv)

    class Unit:
        def __init__(self, src, dst, piece, split, needs):
            self.src, self.dst, self.piece, self.split, self.needs = src, dst, piece, split, needs
            self.z, self.x, self.y, self.dx, self.dy, self.cc = {}, {}, {}, {}, {}, {}

        def ask(self, *steps):
            for r in steps:
                self.z[r] = mv.remote(self.src, self.dst(parts - r), zn[parts - r])

        def first(self, g):
            for k in self.needs[g]:
                self.z[k].wait_recv()
            ref = self.piece(g, q, c, 0, None)
            self.x[g] = mv.remote(ref, ref, xn)
            self.y[g] = mv.remote(ref, ref, yn)
            self.cc[g, 0] = mv.remote(ref, ref, cn)

        def second(self, g):
            self.x[g].wait_recv()
            part = self.split(0, g)
            if part is not None:
                ref = self.piece(g, qx, c, *part)
                self.dy[g] = mv.remote(ref, ref, yn)
            ref = self.piece(g, qx, c, 0, None)
            self.cc[g, 1] = mv.remote(ref, ref, cn)
            self.y[g].wait_recv()
            part = self.split(1, g)
            if part is not None:
                ref = self.piece(g, qy, c, *part)
                self.dx[g] = mv.remote(ref, ref, xn)
            ref = self.piece(g, qy, c, 0, None)
            self.cc[g, 2] = mv.remote(ref, ref, cn)

        def third(self, g):
            for got in (self.dx, self.dy):
                if g in got:
                    got[g].wait_recv()
            ref = self.piece(g, qd, c, 0, None)
            self.cc[g, 3] = mv.remote(ref, ref, cn)

        def last(self, g):
            for k in range(4):
                self.cc[g, k].wait_recv()

    def frozen(src, buf, piece_rows, cut, groups, lead):
        def window(ref, zs, chip, core, off, count):
            count = piece_rows if count is None else count
            at = (zs, pl.ds(chip * piece_rows + off, count), pl.ds(pl.multiple_of(core * half, half), half))
            return ref.at[(slice(None),) * lead + at]

        def own():
            at = (pl.ds(q * piece_rows, piece_rows), pl.ds(pl.multiple_of(c * half, half), half))
            return src.at[(slice(None),) * lead + at]

        return Unit(
            own(),
            lambda k: window(buf, parts - k, q, c, 0, None),
            lambda g, chip, core, off, count: window(buf, groups[g], chip, core, off, count),
            lambda which, g: ((0, cut), (cut, piece_rows - cut))[which],
            {g: (g,) if g else range(1, parts) for g in groups},
        )

    class Total:
        def __init__(self, at, count):
            self.rows, self.lo, self.hi = pl.ds(at, count), pl.ds(0, parts // 2), pl.ds(parts // 2, parts // 2)

        def add(self, dst, src):
            dst[...] = low(dst[...].astype(F32) + src[...].astype(F32))

        def start(self):
            self.core = mv.remote(jbuf.at[:, :, 1 - c, :, self.rows], rc.at[:, :, :, self.rows], cn)

        def step1(self):
            self.core.wait_recv()
            for i in range(2):
                for j in range(2):
                    self.add(jbuf.at[i, j, c, :, self.rows], rc.at[i, j, :, self.rows])
            self.xa = mv.remote(jbuf.at[:, 1 - x, c, self.lo, self.rows], rxa.at[:, :, self.rows], xn)
            self.yb = mv.remote(jbuf.at[1 - y, :, c, self.hi, self.rows], ryb.at[:, :, self.rows], yn)

        def step2(self):
            self.xa.wait_recv()
            self.yb.wait_recv()
            for i in range(2):
                self.add(jbuf.at[i, x, c, self.lo, self.rows], rxa.at[i, :, self.rows])
                self.add(jbuf.at[y, i, c, self.hi, self.rows], ryb.at[i, :, self.rows])
            self.ya = mv.remote(jbuf.at[1 - y, x, c, self.lo, self.rows], rya.at[:, self.rows], yn)
            self.xb = mv.remote(jbuf.at[y, 1 - x, c, self.hi, self.rows], rxb.at[:, self.rows], xn)

        def step3(self):
            self.ya.wait_recv()
            self.xb.wait_recv()
            self.add(jbuf.at[y, x, c, self.lo, self.rows], rya.at[:, self.rows])
            self.add(jbuf.at[y, x, c, self.hi, self.rows], rxb.at[:, self.rows])
            self.zs = []
            for k in range(1, parts):
                src = jbuf.at[y, x, c, lax.rem(z + k, parts), self.rows]
                self.zs.append(mv.remote(src, rz.at[k - 1, self.rows], zn[k]))

        def last(self):
            for copy in self.zs:
                copy.wait_recv()

    heads_rows = wo.shape[1]
    near = (3, 1, 2)
    each = {r: pl.ds(r, 1) for r in near}
    whole = {0: pl.ds(1, parts - 1)}
    u_qkv = frozen(qkv_in, wq, heads_rows // 4, 32, each, 1)
    u_out = frozen(out_in, wo, heads_rows // 4, 16, whole, 0)
    u_up = frozen(up_in, wu, wu.shape[1] // 4, wu.shape[1] // 8, each, 0)
    u_down = frozen(down_in, wd, wd.shape[1] // 4, wd.shape[1] // 8, each, 0)

    def jpiece(g, chip, core, off, count):
        ref = jbuf.at[chip // 2, lax.rem(chip, 2), core, lax.rem(z + g, parts)]
        return ref if count is None else ref.at[pl.ds(off, count)]

    u_join = Unit(
        jbuf.at[y, x, c, z],
        lambda k: jbuf.at[y, x, c, z],
        jpiece,
        lambda which, g: ((0, 48), (48, PLANE - 48))[which],
        {0: (), 1: (1,), 2: (2,), 3: (3,)},
    )

    u_qkv.ask(3, 1)
    l_up = mv.local(aup_in, aup)
    l_dn = mv.local(adn_in, adn)
    l_qkv = mv.local(qkv_in, wq.at[:, 0])
    l_tok = mv.local(tok_in, ct)
    l_out = mv.local(out_in, wo.at[0])
    l_wu = mv.local(up_in, wu.at[0])
    l_wd = mv.local(down_in, wd.at[0])

    gain1, gain2 = flat_row(gain1_in), flat_row(gain2_in)
    spot = lax.broadcasted_iota(jnp.int32, (share, share), 0) == lax.broadcasted_iota(
        jnp.int32, (share, share), 1
    )
    bias_col = jnp.sum(jnp.where(spot, bias_in[...].astype(F32), 0.0), axis=1, keepdims=True)
    l_up.wait()
    m_low = low(nt(jk_in[...], aup[...])).astype(F32)
    own_m[...] = m_low
    part_shift = jnp.sum(bias_col * m_low, axis=0, keepdims=True)
    high = low(part_shift).astype(F32)
    blank = jnp.zeros((PLANE - 3 * share - 2, width), F32)
    tail = jnp.concatenate((high, part_shift - high, blank), axis=0)
    jbuf[y, x, c, z] = low(
        jnp.concatenate((jq_in[...].astype(F32), m_low, jv_in[...].astype(F32), tail), axis=0)
    )
    u_join.first(0)
    u_qkv.first(3)
    u_qkv.first(1)
    u_qkv.ask(2)
    u_out.ask(3, 1, 2)
    u_join.second(0)
    u_qkv.second(3)
    u_qkv.first(2)
    u_up.ask(3, 1)
    u_qkv.second(1)
    u_join.third(0)
    u_out.first(0)
    u_up.ask(2)
    u_qkv.third(3)
    u_qkv.second(2)
    u_qkv.third(1)
    u_up.first(3)
    u_up.first(1)
    u_down.ask(3, 1)
    u_out.second(0)
    u_qkv.third(2)
    for r in near:
        u_qkv.last(r)

    l_tok.wait()
    l_qkv.wait()
    chunks = rows // 128
    seg = seg_in[pl.ds(pl.multiple_of(z * chunks, chunks), chunks), :].astype(F32)
    column = jnp.transpose(seg)
    per_seq = seq_len // 128
    type_f = type_in[...].astype(F32)

    def summed(s):
        rs = pl.ds(s * seq_len, seq_len)
        picks = [column[:, k : k + 1] for k in range(s * per_seq, (s + 1) * per_seq)]
        pick = jnp.concatenate(picks, axis=0) > 0.5
        return ct[rs, :].astype(F32) + jnp.where(pick, type_f[1:2], type_f[0:1])

    xb = jnp.concatenate([low(summed(s)) for s in range(seqs)], axis=0)
    for t in range(3):
        proj[:, t * width : (t + 1) * width] = low(nt(xb, wq[t].reshape(width, width)))
        if t == 0:
            u_out.third(0)
            u_up.first(2)
            u_down.ask(2)
        if t == 1:
            u_up.second(3)
    u_up.second(1)

    pairs = width // (2 * HEAD)
    scale = HEAD ** (-0.5)
    probs_copies = []

    def at_pair(hp, t):
        return pl.ds(pl.multiple_of(t * width + hp * 2 * HEAD, 2 * HEAD), 2 * HEAD)

    def prob_ref(s, hp, h):
        head = hp * 2 + h
        per = width // seq_len
        return (
            head // per,
            pl.ds(s * seq_len, seq_len),
            pl.ds(pl.multiple_of(lax.rem(head, per) * seq_len, seq_len), seq_len),
        )

    places = lax.broadcasted_iota(jnp.int32, (1, seq_len), 1)
    for s in range(seqs):
        rs = pl.ds(s * seq_len, seq_len)
        hidden = jnp.where(places <= ends_in[z * seqs + s], 0.0, NEG)

        def one(hp, carry, s=s, rs=rs, hidden=hidden):
            qp, kp, vp = (proj[rs, at_pair(hp, t)] for t in range(3))
            total = None
            for h in range(2):
                sc = nt(qp, kp * half_mask(h, scale)) + hidden
                e = jnp.exp(sc - jnp.max(sc, axis=1, keepdims=True))
                pb = low(e * (1.0 / jnp.sum(e, axis=1, keepdims=True)))
                big[prob_ref(s, hp, h)] = pb
                term = nn(pb, vp * half_mask(h, 1.0))
                total = term if total is None else total + term
            ctx[rs, at_pair(hp, 0)] = low(total)
            return carry

        lax.fori_loop(0, pairs, one, 0, unroll=3)
        probs_copies.append(mv.local(big.at[:, rs], probs_out.at[:, rs]))
        if s == 0:
            u_up.third(3)
            u_down.first(3)
            u_down.first(1)
            u_join.ask(3, 1)
        if s == 1:
            u_up.second(2)
            u_up.third(1)
            u_down.first(2)
            u_join.ask(2)
        if s == 2:
            u_down.second(3)
            u_up.third(2)
            u_out.last(0)
        if s == 3:
            u_down.second(1)
            u_join.first(3)
            u_join.first(1)
    proj_copy = mv.local(proj, proj_out)

    l_out.wait()
    block = 2 * seq_len
    w_out = wo[...].reshape(width, width)
    for b in range(rows // block):
        rs = pl.ds(b * block, block)
        xs = jnp.concatenate((summed(2 * b), summed(2 * b + 1)), axis=0)
        n, r = normalize(xs + nn(ctx[rs, :], w_out))
        n1[rs, :] = low(n)
        r1[rs, :] = r
        h = n * gain1
        merged[rs, :] = h
        ct[rs, :] = low(h)
    for copy in probs_copies:
        copy.wait()

    l_wu.wait()
    for i, j in enumerate((0,) + near):
        if i == 0:
            u_down.third(3)
            u_join.first(2)
        else:
            u_up.last(j)
        act, slope = gelu_pair(nn(ct[...], wu[j]))
        big[j] = low(act)
        back[j] = low(slope)
        if i == 1:
            u_down.second(2)
            u_down.third(1)
        if i == 2:
            u_join.second(3)
    l_cot = mv.local(cot_in, ct)
    l_wd.wait()
    for i, j in enumerate((0,) + near):
        if i == 1:
            u_down.third(2)
            u_join.second(1)
        if i == 3:
            u_join.third(3)
        if i > 0:
            u_down.last(j)
        merged[...] += nn(big[j], wd[j])
    u_join.third(1)
    u_join.second(2)
    l_dn.wait()
    proj_copy.wait()
    mid_at, slope_at, ku_at = (slice(t * width, (t + 1) * width) for t in range(3))
    mb = low(merged[...])
    big[0] = mb
    mid, slope = gelu_pair(nt(mb, adn[...]))
    proj[:, mid_at], proj[:, slope_at] = low(mid), low(slope)
    u_join.third(2)
    for r in (0,) + near:
        u_join.last(r)

    piece = parts * share

    def pack(i, total):
        planes = [jbuf[i // 4, lax.rem(i // 2, 2), lax.rem(i, 2), k].astype(F32) for k in range(parts)]
        at = pl.ds(pl.multiple_of(i * piece, piece), piece)
        for n, mat in enumerate((qmat, mmat, vmat)):
            mat[at, :] = low(
                jnp.concatenate([pl_[n * share : (n + 1) * share] for pl_ in planes], axis=0)
            )
        for pl_ in planes:
            total += pl_[3 * share : 3 * share + 1] + pl_[3 * share + 1 : 3 * share + 2]
        return total

    shift[...] = lax.fori_loop(0, 8, pack, jnp.zeros((1, width), F32))
    wmat[...] = low(tn(qmat[...], mmat[...]))
    mv.drain()

    units = adapters * bottle
    row_i = lax.broadcasted_iota(jnp.int32, (units, 128), 0)
    lane_i = lax.broadcasted_iota(jnp.int32, (units, 128), 1)
    gather_mat = low(
        jnp.where((row_i >= lane_i * bottle) & (row_i < (lane_i + 1) * bottle), 1.0, 0.0)
    )
    live = lax.broadcasted_iota(jnp.int32, (1, 128), 1) < adapters
    l_cot.wait()
    proj[:, ku_at] = low(nn(big[0], wmat[...]) + shift[...])
    sc = jnp.where(live, nn(proj[:, mid_at] * proj[:, ku_at], gather_mat) * factor, NEG)
    e = jnp.exp(sc - jnp.max(sc, axis=1, keepdims=True))
    jprob[...] = e * (1.0 / jnp.sum(e, axis=1, keepdims=True))
    big[1] = low(nt(low(jprob[...]), gather_mat)) * proj[:, mid_at]
    big[1] = low(merged[...] + nn(big[1], aup[...]))
    merged[...] += nt(big[1], vmat[...])
    out_copies = []
    for b in range(rows // seq_len):
        rs = pl.ds(b * seq_len, seq_len)
        n2, r2 = normalize(merged[rs, :])
        if b >= 2:
            out_copies[b - 2].wait()
        stage[b % 2] = n2 * gain2
        out_copies.append(mv.local(stage.at[b % 2], layer_out.at[rs]))
        gc = norm_back(n2, r2, ct[rs, :].astype(F32) * gain2)
        merged[rs, :] = gc
        big[2, rs, :] = low(gc)
    gm = nn(big[2], vmat[...])
    merged[...] += gm
    big[3] = low(gm)
    big[3] = low(nt(big[3], aup[...]))
    gp = nn(proj[:, mid_at] * big[3], gather_mat)
    jp = jprob[...]
    gs = low(jp * (gp - jnp.sum(jp * gp, axis=1, keepdims=True)) * factor)
    for b in range(rows // block):
        rs = pl.ds(b * block, block)
        at = slice(b * block, (b + 1) * block)
        gs_wide = nt(gs[at], gather_mat)
        jp_wide = nt(low(jp[at]), gather_mat)
        slope = proj[rs, slope_at].astype(F32)
        g_pre = slope * (jp_wide * big[3, rs, :].astype(F32) + gs_wide * proj[rs, ku_at].astype(F32))
        proj[rs, mid_at] = low(gs_wide) * proj[rs, mid_at]
        proj[rs, slope_at] = low(g_pre)
    vmat[...] = low(tn(big[2], big[1]))
    small = jnp.sum(proj[:, mid_at].astype(F32), axis=0, keepdims=True)
    tail = jnp.concatenate((small, jnp.zeros((PLANE - 3 * share - 1, width), F32)), axis=0)

    def lay_first(i, carry):
        at = pl.ds(pl.multiple_of(i * piece, piece), piece)
        mat = vmat[at, :].astype(F32)
        for k in range(parts):
            jbuf[i // 4, lax.rem(i // 2, 2), lax.rem(i, 2), k, 2 * share : PLANE, :] = low(
                jnp.concatenate((mat[k * share : (k + 1) * share], tail), axis=0)
            )
        return carry

    lax.fori_loop(0, 8, lay_first, 0)
    early, late = Total(2 * share, PLANE - 2 * share), Total(0, 2 * share)
    early.start()
    merged[...] += nt(proj[:, mid_at], wmat[...]) + nn(proj[:, slope_at], adn[...])
    for copy in out_copies[-2:]:
        copy.wait()

    rb = low(tn(proj[:, mid_at], big[0]))
    early.step1()
    wmat[...] = low(nn(mmat[...], rb))
    inner = low(nt(rb, qmat[...]))
    qmat[...] = low(tn(inner, aup[...]))

    def lay(i, carry):
        at = pl.ds(pl.multiple_of(i * piece, piece), piece)
        mats = [mat[at, :].astype(F32) for mat in (wmat, qmat)]
        for k in range(parts):
            jbuf[i // 4, lax.rem(i // 2, 2), lax.rem(i, 2), k, 0 : 2 * share, :] = low(
                jnp.concatenate([m[k * share : (k + 1) * share] for m in mats], axis=0)
            )
        return carry

    lax.fori_loop(0, 8, lay, 0)
    late.start()
    probs_back = mv.local(probs_out, big)
    proj_back = mv.local(proj_out, proj)

    ct[...] = low(merged[...])
    for j in range(parts):
        back[j] = low(nt(ct[...], wd[j]) * back[j].astype(F32))
        if j == 1:
            early.step2()
            late.step1()
    for b in range(rows // block):
        rs = pl.ds(b * block, block)
        total = merged[rs, :]
        for j in range(parts):
            total += nt(back[j, rs, :], wu[j])
        g_sum = norm_back(n1[rs, :].astype(F32), r1[rs, :], total * gain1)
        merged[rs, :] = g_sum
        back[0, rs, :] = low(nt(low(g_sum), w_out))
        if b == 0:
            early.step3()
    late.step2()
    probs_back.wait()
    proj_back.wait()

    grad_copies = []
    for s in range(seqs):
        rs = pl.ds(s * seq_len, seq_len)

        def one_back(hp, carry, s=s, rs=rs):
            qp, kp, vp = (proj[rs, at_pair(hp, t)] for t in range(3))
            go = back[0, rs, at_pair(hp, 0)]
            both = go.astype(F32) * ctx[rs, at_pair(hp, 0)].astype(F32)
            gq = gk = gv = None
            for h in range(2):
                mask, mask_s = half_mask(h, 1.0), half_mask(h, scale)
                pb = big[prob_ref(s, hp, h)]
                delta = jnp.sum(both * mask.astype(F32), axis=1, keepdims=True)
                ds = low(pb.astype(F32) * (nt(go, vp * mask) - delta))
                terms = nn(ds, kp * mask_s), tn(ds, qp * mask_s), tn(pb, go * mask)
                gq, gk, gv = terms if gq is None else (gq + terms[0], gk + terms[1], gv + terms[2])
            for t, g in enumerate((gq, gk, gv)):
                proj[rs, at_pair(hp, t)] = low(g)
            return carry

        lax.fori_loop(0, pairs, one_back, 0, unroll=6)
        if s == 1:
            late.step3()
        if s % 2 == 1:
            b = s // 2
            rs = pl.ds(b * block, block)
            total = merged[rs, :]
            for t in range(3):
                total += nn(proj[rs, t * width : (t + 1) * width], wq[t].reshape(width, width))
            merged[rs, :] = total
            grad_copies.append(mv.local(merged.at[rs], grad_out.at[rs]))

    early.last()
    late.last()
    total = jbuf[y, x, c, z].astype(F32)
    for k in range(1, parts):
        total += rz[k - 1].astype(F32)
    flow = total[3 * share : 3 * share + 8]
    turned = nn(low(flow), aup[...])
    key_part = total[share : 2 * share] + bias_col * turned[0:1]
    g_bias = jnp.sum(own_m[...] * flow[0:1], axis=1, keepdims=True)
    join_out[0:share, :] = total[0:share]
    join_out[share : 2 * share, :] = key_part
    join_out[2 * share : 3 * share, :] = total[2 * share : 3 * share]
    wide = jnp.where(
        lax.broadcasted_iota(jnp.int32, (share, 128), 0)
        == lax.broadcasted_iota(jnp.int32, (share, 128), 1),
        g_bias,
        0.0,
    )
    bias_out[...] = jnp.broadcast_to(jnp.sum(wide, axis=0, keepdims=True), (8, 128))
    mv.drain()
    for copy in grad_copies:
        copy.wait()


def hand_over(
    layer_in, grad_in, join_in, bias_in,
    layer_out, grad_out, gq_out, gk_out, gv_out, bias_out,
    held, turned, arrive, leave,
):
    rows, share = layer_in.shape[0] // 4, gq_out.shape[0]
    steps = []
    for n, (src, dst) in enumerate(((layer_in, layer_out), (grad_in, grad_out))):
        for i in range(4):
            at = pl.ds(i * rows, rows)
            steps.append((src.at[at], held.at[n, at], dst.at[at]))
    for i, dst in enumerate((gq_out, gk_out, gv_out)):
        steps.append((join_in.at[pl.ds(i * share, share)], turned.at[i], dst))
    inward = [pltpu.make_async_copy(s, m, arrive.at[i]) for i, (s, m, _) in enumerate(steps)]
    outward = [pltpu.make_async_copy(m, d, leave.at[i]) for i, (_, m, d) in enumerate(steps)]
    for copy in inward:
        copy.start()
    bias_out[...] = bias_in[0:1, 0:share]
    for came, goes in zip(inward, outward):
        came.wait()
        goes.start()
    for copy in outward:
        copy.wait()


def local(
    tokens,
    segment_ids,
    row_ends,
    type_rows,
    ln1_gain,
    attn_qkv,
    attn_out,
    ffn_up,
    ffn_down,
    adapter_down,
    adapter_up,
    ln2_gain,
    joining_query,
    joining_key,
    joining_value,
    query_bias,
    cotangent,
):
    dp, parts = lax.axis_size("dp"), lax.axis_size("mp")
    dpi, z = lax.axis_index("dp"), lax.axis_index("mp")
    rows, width = tokens.shape
    seqs = row_ends.shape[0] // parts
    seq_len = rows // seqs
    adapters, _, bottle = adapter_down.shape
    share = width // (8 * parts)
    axes = ("dp", "mp")

    joins = (joining_query, joining_key, joining_value)
    bias = query_bias
    if dp > 8:
        at = (lax.rem(dpi, 8) * parts + z) * share
        joins = tuple(
            lax.dynamic_slice_in_dim(lax.all_gather(m, axes, axis=1, tiled=True), at, share, 1)
            for m in joins
        )
        bias = lax.dynamic_slice_in_dim(lax.all_gather(bias, axes, axis=0, tiled=True), at, share, 0)
    qkv_in = jnp.transpose(attn_qkv, (0, 2, 1))

    cols = attn_qkv.shape[2]
    ff = ffn_up.shape[1]
    dims = (rows, width, seqs, seq_len, parts, adapters, bottle, share)
    mat = pltpu.VMEM((width, width), BF)
    any_, vm = pl.BlockSpec(memory_space=pl.ANY), pl.BlockSpec(memory_space=pltpu.VMEM)
    sm = pl.BlockSpec(memory_space=pltpu.SMEM)
    planes = lambda *lead: pltpu.VMEM(lead + (PLANE, width), BF)
    out = pl.pallas_call(
        functools.partial(kernel, dims),
        out_shape=(
            jax.ShapeDtypeStruct((rows, width), F32),
            jax.ShapeDtypeStruct((rows, width), F32),
            jax.ShapeDtypeStruct((3 * share, width), F32),
            jax.ShapeDtypeStruct((8, 128), F32),
            jax.ShapeDtypeStruct((parts, rows, width), BF),
            jax.ShapeDtypeStruct((rows, 3 * width), BF),
        ),
        in_specs=[any_, any_, vm, sm, vm, vm, vm, vm, any_, any_, any_, any_, any_, any_, vm, vm, vm],
        out_specs=(any_, any_, vm, vm, any_, any_),
        scratch_shapes=[
            pltpu.VMEM((3, parts, cols, width), BF),
            pltpu.VMEM((parts, cols, width), BF),
            pltpu.VMEM((parts, width, ff), BF),
            pltpu.VMEM((parts, ff, width), BF),
            mat, mat, mat, mat, mat, mat,
            pltpu.VMEM((1, width), F32),
            planes(2, 2, 2, parts),
            planes(2, 2, parts),
            planes(2, parts // 2),
            planes(2, parts // 2),
            planes(parts // 2),
            planes(parts // 2),
            planes(parts - 1),
            pltpu.VMEM((rows, width), BF),
            pltpu.VMEM((rows, 3 * width), BF),
            pltpu.VMEM((parts, rows, ff), BF),
            pltpu.VMEM((parts, rows, ff), BF),
            pltpu.VMEM((rows, width), BF),
            pltpu.VMEM((rows, width), BF),
            pltpu.VMEM((rows, 1), F32),
            pltpu.VMEM((rows, width), F32),
            pltpu.VMEM((2, seq_len, width), F32),
            pltpu.VMEM((rows, 128), F32),
            pltpu.VMEM((share, width), F32),
            pltpu.SemaphoreType.DMA((192,)),
            pltpu.SemaphoreType.DMA((192,)),
        ],
        compiler_params=pltpu.CompilerParams(
            collective_id=0, has_side_effects=True, vmem_limit_bytes=VMEM_LIMIT
        ),
    )(
        tokens, cotangent, segment_ids.reshape(-1, 128), row_ends, type_rows,
        ln1_gain.reshape(-1, 128), ln2_gain.reshape(-1, 128), bias[None, :], qkv_in, attn_out, ffn_up, ffn_down,
        jnp.transpose(adapter_down, (0, 2, 1)).reshape(adapters * bottle, width),
        adapter_up.reshape(adapters * bottle, width), *(jnp.transpose(m) for m in joins),
    )
    layer_out, g_in, grads, g_bias, _, _ = out
    layer_out, g_in, *grads, g_bias = pl.pallas_call(
        hand_over,
        out_shape=tuple(
            jax.ShapeDtypeStruct((n, width), F32) for n in (rows, rows, share, share, share)
        )
        + (jax.ShapeDtypeStruct((1, share), F32),),
        in_specs=[any_] * 3 + [vm],
        out_specs=(any_,) * 5 + (vm,),
        scratch_shapes=[
            pltpu.VMEM((2, rows, width), F32),
            pltpu.VMEM((3, share, width), F32),
            pltpu.SemaphoreType.DMA((11,)),
            pltpu.SemaphoreType.DMA((11,)),
        ],
        compiler_params=pltpu.CompilerParams(vmem_limit_bytes=VMEM_LIMIT),
    )(layer_out, g_in, grads, g_bias)
    g_bias = g_bias[0]
    if dp > 8:
        at = (lax.rem(dpi, 8) * parts + z) * share
        own, first = width // (dp * parts), (dpi * parts + z) * (width // (dp * parts))
        whole = lambda v, axis: lax.psum(
            lax.dynamic_update_slice_in_dim(
                jnp.zeros(v.shape[:axis] + (width,) + v.shape[axis + 1 :], F32), v, at, axis
            ),
            axes,
        )
        grads = lax.dynamic_slice_in_dim(whole(jnp.stack(grads), 1), first, own, 1)
        g_bias = lax.dynamic_slice_in_dim(whole(g_bias, 0), first, own, 0)
    g_q, g_k, g_v = (jnp.transpose(grads[i]) for i in range(3))
    return (layer_out, g_in, g_q, g_k, g_v, g_bias)


VMEM_LIMIT = 63 * 1024 * 1024


def solution(mesh):
    in_specs = (
        P(("dp", "mp"), None),
        P("dp"),
        P("dp"),
        P(),
        P(),
        P(None, None, "mp"),
        P("mp", None),
        P(None, "mp"),
        P("mp", None),
        P(),
        P(),
        P(),
        P(None, ("dp", "mp")),
        P(None, ("dp", "mp")),
        P(None, ("dp", "mp")),
        P(("dp", "mp")),
        P(("dp", "mp"), None),
    )
    out_specs = (
        P(("dp", "mp"), None),
        P(("dp", "mp"), None),
        P(None, ("dp", "mp")),
        P(None, ("dp", "mp")),
        P(None, ("dp", "mp")),
        P(("dp", "mp")),
    )
    return jax.shard_map(local, mesh=mesh, in_specs=in_specs, out_specs=out_specs, check_vma=False)
```
